32 devices in a mesh: ctx: 16 (over z, y, core), tp: 2 (over x).
Axes of the slice: x: 2, y: 2, z: 4, core: 2. Of those that a mesh axis runs over, the one named last changes fastest.
Arguments:
- inputs: float32 [4096, 5120], P('ctx', 'tp'), may hold values from -6 to 6
- state_input: float32 [4096, 128], P('ctx'), may hold values from -0.125 to 0.125
- state_output: float32 [4096, 128], P('ctx'), may hold values from -0.125 to 0.125
- decay_codes: int32 [80, 4096], P('tp', 'ctx'), may hold values from 0 to 45000
- output_grad: float32 [4096, 5120], P('ctx', 'tp'), may hold values from -6 to 6
Outputs:
- input_grad: float32 [4096, 5120], P('ctx', 'tp')
- b_grad: float32 [4096, 128], P(('ctx', 'tp'))
- c_grad: float32 [4096, 128], P(('ctx', 'tp'))
- decay_grad: float32 [80, 4096], P('tp', 'ctx')
The draws below stay inside these ranges and needn't reach their ends.
All inputs are finite; a program needn't handle non-finite values.
Results may differ from the reference program's by a relative error of at most 0.00029.
Values sent between devices are 32-bit elements; how exact they have to be, the bound alone decides.
A program may use at most 128 MiB of HBM per device.

```python
import jax
import jax.numpy as jnp
from jax import lax

HEAD_TOTAL = 80
P_SIZE = 64
N = 128
Q = 256
TOK_DEV = 256
SEQUENCE_TOTAL = 4096


def draw_decay_codes(key, part):
    segment_keys = jax.random.split(key, 11)
    total_length = SEQUENCE_TOTAL
    block_total = total_length // TOK_DEV
    base_cap = 16384 // total_length
    high_code = max(2, 196608 // total_length)
    medium_low = max(1, 737280 // total_length)
    run_total = total_length // 48 + 2
    head_class = jax.random.randint(segment_keys[0], (HEAD_TOTAL, 1), 0, 4)
    multiplier = jax.random.randint(segment_keys[1], (HEAD_TOTAL, block_total, 1), 1, 4)
    multiplier = jnp.broadcast_to(multiplier, (HEAD_TOTAL, block_total, TOK_DEV)).reshape(HEAD_TOTAL, total_length)
    fast_blocks = jax.random.randint(segment_keys[6], (HEAD_TOTAL, block_total, 1), 0, 4)
    fast_blocks = jnp.broadcast_to(fast_blocks, (HEAD_TOTAL, block_total, TOK_DEV)).reshape(HEAD_TOTAL, total_length)
    base_codes = jax.random.randint(segment_keys[2], (HEAD_TOTAL, total_length), 0, 1 << 20) % (multiplier * base_cap + 1)
    run_gaps = jax.random.randint(segment_keys[7], (HEAD_TOTAL, run_total), 40, 153)
    run_lengths = jax.random.randint(segment_keys[8], (HEAD_TOTAL, run_total), 12, 37)
    run_phase = jax.random.randint(segment_keys[9], (HEAD_TOTAL, 1), 0, 96)
    run_ends = jnp.cumsum(run_gaps + run_lengths, axis=1) - run_phase
    run_starts = run_ends - run_lengths
    run_starts = jnp.minimum(jnp.maximum(run_starts, 0), total_length)
    run_ends = jnp.minimum(jnp.maximum(run_ends, 0), total_length)
    head_rows = lax.broadcasted_iota(jnp.int32, (HEAD_TOTAL, run_total), 0)
    run_marks = jnp.zeros((HEAD_TOTAL, total_length + 1), jnp.int32)
    run_marks = run_marks.at[head_rows, run_starts].add(1)
    run_marks = run_marks.at[head_rows, run_ends].add(-1)
    high_here = jnp.cumsum(run_marks, axis=1)[:, :total_length]
    slow_codes = base_codes + high_here * high_code
    medium_codes = jax.random.randint(segment_keys[10], (HEAD_TOTAL, total_length), medium_low, medium_low + medium_low // 9 + 1)
    fast_codes = jax.random.randint(segment_keys[3], (HEAD_TOTAL, total_length), 1300, 2201)
    surge_offsets = jax.random.randint(segment_keys[4], (HEAD_TOTAL, 2), 0, total_length)
    surge_lengths = jax.random.randint(segment_keys[5], (HEAD_TOTAL, 2), 14600, 45001)
    surge_lengths = surge_lengths.at[0, 0].set(45000)
    position_grid = lax.broadcasted_iota(jnp.int32, (HEAD_TOTAL, total_length), 1)
    surge_spans = jnp.max(jnp.where(position_grid[:, :, None] == surge_offsets[:, None, :], surge_lengths[:, None, :], 0), axis=-1)
    fast_here = jnp.logical_and(head_class == 2, fast_blocks == 0)
    uniform_rate = jnp.where(head_class == 3, medium_codes, jnp.where(fast_here, fast_codes, slow_codes))
    return jnp.where(surge_spans > 0, surge_spans, uniform_rate).astype(jnp.int32)


def shard_levels(rng, shape, cuts, low, largest):
    def one(position, parts):
        heights = jax.random.uniform(jax.random.fold_in(jax.random.fold_in(rng, 6), position), (parts,), jnp.float32, low / len(cuts), largest / len(cuts))
        return jnp.repeat(jnp.exp(heights), shape[position] // parts).reshape((-1,) + (1,) * (len(shape) - position - 1))

    level = one(*cuts[0])
    for cut in cuts[1:]:
        level = level * one(*cut)
    return level


def noise(rng, shape, deviation, reach, shards=(), held_as=jnp.bfloat16):
    entries = jax.random.normal(rng, shape, jnp.float32) * deviation
    if len(shards) > 0:
        entries = shard_levels(rng, shape, shards, -0.22, 0.18) * entries
    return jnp.clip(entries, min=-reach, max=reach).astype(held_as)


def setup_inputs(seed: int = 0) -> dict:
    splits = jax.random.split(jax.random.key(seed), 6)
    return {
        "inputs": noise(splits[0], (SEQUENCE_TOTAL, HEAD_TOTAL * P_SIZE), 1.0, 6.0, ((0, 16), (1, 2)), jnp.float32),
        "state_input": noise(splits[1], (SEQUENCE_TOTAL, N), (16 * N) ** -0.5, 0.125, ((0, 16),), jnp.float32),
        "state_output": noise(splits[2], (SEQUENCE_TOTAL, N), (16 * N) ** -0.5, 0.125, ((0, 16),), jnp.float32),
        "decay_codes": draw_decay_codes(jax.random.fold_in(splits[5], 71), 0),
        "output_grad": noise(splits[4], (SEQUENCE_TOTAL, HEAD_TOTAL * P_SIZE), 1.0, 6.0, ((0, 16), (1, 2)), jnp.float32),
    }


PRECISE = lax.Precision.HIGHEST
CODE_UNIT = 2.0 ** (-16)

def decay_parts(log_decay):
    within = jnp.cumsum(log_decay, axis=-1)
    return (within, within[..., -1])

def block_states(values, writers, within, final_log):
    tail_decay = jnp.exp(final_log[..., None] - within)
    return jnp.einsum('hks,hksp,ksn->hkpn', tail_decay, values, writers, precision=PRECISE)

def fold_blocks(start_state, factors, pieces):

    def carry_step(carried_state, element):
        factor, portion = element
        return (factor[:, None, None] * carried_state + portion, carried_state)
    return lax.scan(carry_step, start_state, (jnp.moveaxis(factors, 1, 0), jnp.moveaxis(pieces, 1, 0)))

def ssd_forward(values, writers, readers, log_decay, start_state):
    within, final_log = decay_parts(log_decay)
    row_index = lax.broadcasted_iota(jnp.int32, (Q, Q), 0)
    column_index = lax.broadcasted_iota(jnp.int32, (Q, Q), 1)
    causal = column_index <= row_index
    log_gap = within[..., :, None] - within[..., None, :]
    decay_matrix = jnp.where(causal, jnp.exp(jnp.where(causal, log_gap, 0.0)), 0.0)
    scores = jnp.einsum('ktn,ksn->kts', readers, writers, precision=PRECISE)
    intra_out = jnp.einsum('hkts,hksp->hktp', decay_matrix * scores[None], values, precision=PRECISE)
    pieces = block_states(values, writers, within, final_log)
    end_state, entering = fold_blocks(start_state, jnp.exp(final_log), pieces)
    entering = jnp.moveaxis(entering, 0, 1)
    inter_out = jnp.exp(within)[..., None] * jnp.einsum('ktn,hkpn->hktp', readers, entering, precision=PRECISE)
    return (intra_out + inter_out, end_state)

def reference(inputs, state_input, state_output, decay_codes, output_grad):
    block_count = SEQUENCE_TOTAL // Q
    head_inputs = jnp.transpose(inputs.reshape(SEQUENCE_TOTAL, HEAD_TOTAL, P_SIZE), (1, 0, 2)).reshape(HEAD_TOTAL, 1, block_count, Q, P_SIZE)
    head_grads = jnp.transpose(output_grad.reshape(SEQUENCE_TOTAL, HEAD_TOTAL, P_SIZE), (1, 0, 2)).reshape(HEAD_TOTAL, 1, block_count, Q, P_SIZE)
    log_decay = (-decay_codes.astype(jnp.float32) * CODE_UNIT).reshape(HEAD_TOTAL, 1, block_count, Q)
    writers = state_input.reshape(block_count, Q, N)
    readers = state_output.reshape(block_count, Q, N)
    empty_state = jnp.zeros((1, P_SIZE, N), jnp.float32)

    def one_head(sums, element):
        values, cotangent, decay_row = element

        def forward(values_in, writers_in, readers_in, decay_in):
            return ssd_forward(values_in, writers_in, readers_in, decay_in, empty_state)[0]
        _, pullback = jax.vjp(forward, values, writers, readers, decay_row)
        grad_values, grad_writers, grad_readers, grad_decay = pullback(cotangent)
        return ((sums[0] + grad_writers, sums[1] + grad_readers), (grad_values[0], grad_decay[0]))
    start_sums = (jnp.zeros((block_count, Q, N), jnp.float32), jnp.zeros((block_count, Q, N), jnp.float32))
    (writer_grad, reader_grad), (value_grad, decay_grad) = lax.scan(one_head, start_sums, (head_inputs, head_grads, log_decay))
    input_grad = jnp.transpose(value_grad.reshape(HEAD_TOTAL, SEQUENCE_TOTAL, P_SIZE), (1, 0, 2)).reshape(SEQUENCE_TOTAL, HEAD_TOTAL * P_SIZE)
    return (input_grad, writer_grad.reshape(SEQUENCE_TOTAL, N), reader_grad.reshape(SEQUENCE_TOTAL, N), decay_grad.reshape(HEAD_TOTAL, SEQUENCE_TOTAL))
```

```python
import functools

import jax
import jax.numpy as jnp
from jax import lax
from jax.experimental import pallas as pl
from jax.experimental.pallas import tpu as pltpu
from jax.sharding import PartitionSpec as P

MESH = pl.DeviceIdType.MESH
CODE_UNIT = 2.0 ** (-16)
LANES = 128
HALF = 64
F32 = jnp.float32
BF16 = jnp.bfloat16
NN = (((1,), (0,)), ((), ()))
NT = (((1,), (1,)), ((), ()))
TN = (((0,), (0,)), ((), ()))


def dot(a, b, dims=NN):
    return lax.dot_general(a, b, dims, preferred_element_type=F32)


def parts(a):
    high = a.astype(BF16)
    return high, (a - high.astype(F32)).astype(BF16)


def exact_dot(a, ones, dims):
    first = a.astype(BF16)
    rest = a - first.astype(F32)
    second = rest.astype(BF16)
    third = (rest - second.astype(F32)).astype(BF16)
    return dot(first, ones, dims) + dot(second, ones, dims) + dot(third, ones, dims)


def swap(a):
    return pltpu.roll(a, HALF, 1)


def kernel(
    ctx, tp, x_ref, b_ref, c_ref, code_ref, g_ref,
    dx_ref, db_ref, dc_ref, da_ref,
    wl, loc, dec, rdec0, dec1, rdec1, rbuf0, agg, rbuf1, zin, zout, zp, snd1, snd0, ent,
    score, dscore, rows_acc, col_acc, colq_acc, bc, rtp,
    cwide, bwide, send, recv,
):
    heads, toks = code_ref.shape
    pairs = x_ref.shape[1] // LANES
    two = pairs % 2 == 0
    four = pairs % 4 == 0
    hp = pairs // 2 if two else pairs
    qp = pairs // 4 if four else hp
    group = 4 if four else 2 if two else 1
    groups = ctx // group
    mid = toks // 2

    me = lax.axis_index("ctx")
    my_tp = lax.axis_index("tp")
    place = me // group
    core = me % 2 if two else 0
    side = (me // 2) % 2 if four else 0
    core_mate = me + 1 - 2 * (me % 2)
    side_mate = me + 2 - 4 * ((me // 2) % 2)
    half0 = core * hp if two else 0
    mine0 = side * qp if four else 0

    n_dec1 = 3
    n_up = 4
    n_chain = n_up + 2 * qp
    n_down = n_chain + 2 * qp
    n_last = n_down + 2 * qp
    n_tp = n_last + 2 * hp

    def copy(src, dst, number, to):
        return pltpu.make_async_remote_copy(
            src_ref=src, dst_ref=dst, send_sem=send.at[number], recv_sem=recv.at[number],
            device_id=to, device_id_type=MESH,
        )

    def up0(d):
        there = (1 - core) * hp
        return copy(loc.at[d, pl.ds(there, hp)], rbuf0.at[d], d, {"ctx": core_mate})

    def dec0_copy():
        return copy(dec, rdec0, 2, {"ctx": core_mate})

    def dec1_copy():
        return copy(dec1, rdec1, n_dec1, {"ctx": side_mate})

    def up1(d, k):
        return copy(
            agg.at[d, (1 - side) * qp + k], rbuf1.at[d, k], n_up + d * qp + k, {"ctx": side_mate}
        )

    def chain(d, k):
        to = me + group if d == 0 else me - group
        return copy(zout.at[d, k], zin.at[d, k], n_chain + d * qp + k, {"ctx": to})

    def down1(d, k):
        return copy(
            snd1.at[d, k], zp.at[d, mine0 + k], n_down + d * qp + k, {"ctx": side_mate}
        )

    def down0(d, k):
        return copy(
            snd0.at[d, k], ent.at[d, half0 + k], n_last + d * hp + k, {"ctx": core_mate}
        )

    rt = toks // tp

    def tp_copy(step):
        to = lax.rem(my_tp + step, tp)
        return copy(
            bc.at[:, pl.ds(pl.multiple_of(to * rt, rt), rt)], rtp.at[step - 1],
            n_tp + step - 1, {"tp": to},
        )

    barrier = pltpu.get_barrier_semaphore()

    def greet(to):
        pl.semaphore_signal(barrier, inc=1, device_id=to, device_id_type=MESH)

    expected = tp - 1
    if two:
        greet({"ctx": core_mate})
        expected = expected + 1
    if four:
        greet({"ctx": side_mate})
        expected = expected + 1
    for step in range(1, tp):
        greet({"tp": lax.rem(my_tp + step, tp)})

    @pl.when(place > 0)
    def _():
        greet({"ctx": me - group})

    @pl.when(place < groups - 1)
    def _():
        greet({"ctx": me + group})

    inner = jnp.where(place > 0, 1, 0) + jnp.where(place < groups - 1, 1, 0)

    row_i = lax.broadcasted_iota(jnp.int32, (toks, toks), 0)
    col_i = lax.broadcasted_iota(jnp.int32, (toks, toks), 1)
    low_left = lax.broadcasted_iota(jnp.int32, (toks, LANES), 1) < HALF
    left_mid = lax.broadcasted_iota(jnp.int32, (mid, LANES), 1) < HALF
    lane = lax.broadcasted_iota(jnp.int32, (toks, LANES), 1)

    def cols(q):
        return pl.ds(pl.multiple_of(q * LANES, LANES), LANES)

    codes = code_ref[...]
    code_high = lax.shift_right_logical(codes, 8).astype(F32)
    code_low = (codes & 255).astype(F32)
    upto = (col_i <= row_i).astype(BF16)
    run_high = dot(upto, code_high.astype(BF16), NT)
    run_low = dot(upto, code_low.astype(BF16), NT)
    total = run_high * 256.0 + run_low
    within_col = total * (-CODE_UNIT)

    head_row = lax.broadcasted_iota(jnp.int32, (heads, toks), 0)
    del head_row
    rows_acc[...] = jnp.zeros_like(rows_acc)
    rows_acc[0:heads, :] = (
        dot(code_high.astype(BF16), (row_i <= col_i).astype(BF16)) * 256.0
        + dot(code_low.astype(BF16), (row_i <= col_i).astype(BF16))
    ) * (-CODE_UNIT)
    for q in range(pairs):
        wl[:, q * LANES:(q + 1) * LANES] = jnp.where(
            low_left, within_col[:, 2 * q:2 * q + 1], within_col[:, 2 * q + 1:2 * q + 2]
        )
    dec[...] = jnp.zeros_like(dec)
    for q in range(pairs):
        dec[q:q + 1, :] = jnp.exp(wl[toks - 1:toks, q * LANES:(q + 1) * LANES])

    b_high, b_low = parts(b_ref[...])
    c_high, c_low = parts(c_ref[...])
    bwide[...] = jnp.concatenate([b_high, b_low], axis=1)
    cwide[...] = jnp.concatenate([c_high, c_low], axis=1)
    b_tall = jnp.transpose(jnp.concatenate([b_high.astype(F32), b_low.astype(F32)], axis=1)).astype(BF16)
    c_tall = jnp.transpose(jnp.concatenate([c_high.astype(F32), c_low.astype(F32)], axis=1)).astype(BF16)

    def weighted(q):
        w = wl[:, cols(q)]
        tail = jnp.exp(wl[pl.ds(toks - 1, 1), cols(q)] - w)
        return tail, jnp.exp(w)

    def local_state(q):
        tail, head = weighted(q)
        for d, (tall, value) in enumerate(
            ((b_tall, tail * x_ref[:, cols(q)]), (c_tall, head * g_ref[:, cols(q)]))
        ):
            high, low = parts(value)
            out = dot(tall, jnp.concatenate([high, low], axis=1))
            out = out[:LANES] + out[LANES:]
            loc[d, q] = out[:, :LANES] + out[:, LANES:]

    def loop(count, body):
        lax.fori_loop(0, count, lambda k, _: (body(k), 0)[1], 0)

    if two:
        loop(hp, lambda k: local_state((1 - core) * hp + k))
    else:
        loop(hp, local_state)
    pl.semaphore_wait(barrier, expected + inner)
    if two:
        dec0_copy().start()
        up0(0).start()
        up0(1).start()
        loop(hp, lambda k: local_state(half0 + k))

    score[...] = (
        dot(b_high, c_high, NT) + dot(b_high, c_low, NT) + dot(b_low, c_high, NT)
    )
    dscore[...] = jnp.zeros_like(dscore)
    col_acc[...] = jnp.zeros_like(col_acc)
    colq_acc[...] = jnp.zeros_like(colq_acc)
    bc[...] = jnp.zeros_like(bc)
    causal = row_i <= col_i

    def intra(q):
        x = x_ref[:, cols(q)]
        g = g_ref[:, cols(q)]
        w = wl[:, cols(q)]
        xh = x.astype(BF16).astype(F32)
        xl = x - xh
        gh = g.astype(BF16).astype(F32)
        gl = g - gh
        xl_s, gh_s, gl_s, w_s = swap(xl), swap(gh), swap(gl), swap(w)
        xh_b, gh_b = xh.astype(BF16), gh.astype(BF16)
        zero = jnp.zeros_like(g)
        results = []
        for n in range(2):
            if n == 0:
                pick = lambda a, b: jnp.where(low_left, a, b)
            else:
                pick = lambda a, b: jnp.where(low_left, b, a)
            left = jnp.concatenate([pick(xh, xl_s).astype(BF16), xh_b], axis=1)
            right = jnp.concatenate([pick(gh, gh_s).astype(BF16), pick(gl, zero).astype(BF16)], axis=1)
            value = pick(gh, gl_s).astype(BF16)
            w_here = pick(w, w_s)
            row = rows_acc[pl.ds(2 * q + n, 1), :]
            out = []
            colsum = []
            rowsum = []
            for r in range(2):
                here = slice(r * mid, (r + 1) * mid)
                after = slice(r * mid, toks)
                width = toks - r * mid
                wh = w_here[here]
                wide = jnp.concatenate([wh] * (width // LANES), axis=1)
                gap = jnp.where(causal[here, after], row[:, after] - wide, -1e30)
                decay = jnp.exp(gap)
                dm = dot(left[here], right[after], NT)
                scaled = dm * decay
                sc = score[here, after]
                dscore[here, after] += scaled
                z = scaled * sc
                colsum.append(jnp.sum(z, axis=0, keepdims=True))
                rowsum.append(jnp.sum(z, axis=1, keepdims=True))
                mh, ml = parts(decay * sc)
                main = dot(mh, value[after])
                out.append(main + swap(main) + dot(ml, gh_b[after]))
            results.append(jnp.concatenate(out, axis=0))
            rows_acc[pl.ds(2 * q + n, 1), :] = jnp.concatenate(
                [colsum[0][:, :mid], colsum[0][:, mid:] + colsum[1]], axis=1
            )
            col_acc[...] -= jnp.where(lane == 2 * q + n, jnp.concatenate(rowsum, axis=0), 0.0)
        dx_ref[:, cols(q)] = jnp.where(low_left, results[0], results[1])

    ticks = groups - 1 + qp
    early = pairs // 5
    loop(early, intra)

    if two:
        dec0_copy().wait()
        up0(0).wait()
        up0(1).wait()
        dec1[...] = dec[...] * rdec0[...]

        def join(d, k):
            own_first = core == d
            q = half0 + k
            one = jnp.ones((1, LANES), F32)
            mine, other = dec[pl.ds(q, 1), :], rdec0[pl.ds(q, 1), :]
            agg[d, k] = (
                jnp.where(own_first, other, one) * loc[d, q]
                + jnp.where(own_first, one, mine) * rbuf0[d, k]
            )

        if four:
            dec1_copy().start()

            def out_up(k):
                for d in range(2):
                    join(d, (1 - side) * qp + k)
                    up1(d, k).start()

            loop(qp, out_up)

        def keep(k):
            for d in range(2):
                join(d, mine0 + k)

        loop(qp, keep)
    else:
        dec1[...] = dec[...]

        def keep(k):
            for d in range(2):
                agg[d, k] = loc[d, k]

        loop(qp, keep)
    if four:
        dec1_copy().wait()

    def finish_core(d, k):
        q = half0 + k
        z = zp[d, k]
        if not two:
            ent[d, q] = z
            return
        own_first = core == d
        first_dec = jnp.where(own_first, dec[pl.ds(q, 1), :], rdec0[pl.ds(q, 1), :])
        first = jnp.where(own_first, loc[d, q], rbuf0[d, k])
        later = first_dec * z + first
        ent[d, q] = jnp.where(own_first, z, later)
        snd0[d, k] = jnp.where(own_first, later, z)
        down0(d, k).start()

    def carry(d, k):
        q = half0 + mine0 + k
        has_before = place > 0 if d == 0 else place < groups - 1
        has_after = place < groups - 1 if d == 0 else place > 0
        own = agg[d, mine0 + k]
        mine = dec1[pl.ds(q, 1), :]
        if four:
            up1(d, k).wait_recv()
            other = rdec1[pl.ds(q, 1), :]
            got = rbuf1[d, k]
            own_first = side == d
            one = jnp.ones((1, LANES), F32)
            full = jnp.where(own_first, other, one) * own + jnp.where(own_first, one, mine) * got
            full_dec = mine * other
        else:
            full, full_dec = own, mine

        @pl.when(has_before)
        def _():
            chain(d, k).wait_recv()

        @pl.when(jnp.logical_not(has_before))
        def _():
            zin[d, k] = jnp.zeros((LANES, LANES), F32)

        z = zin[d, k]

        @pl.when(has_after)
        def _():
            zout[d, k] = full_dec * z + full
            chain(d, k).start()

        if four:
            first_dec = jnp.where(own_first, mine, other)
            later = first_dec * z + jnp.where(own_first, own, got)
            snd1[d, k] = jnp.where(own_first, later, z)
            down1(d, k).start()
            zp[d, mine0 + k] = jnp.where(own_first, z, later)
        else:
            zp[d, mine0 + k] = z
        finish_core(d, mine0 + k)

    per = -(-(pairs - early) // ticks)

    def tick(t):
        for d in range(2):
            k = t - place if d == 0 else t - (groups - 1 - place)

            @pl.when(jnp.logical_and(k >= 0, k < qp))
            def _():
                carry(d, k)

        for j in range(per):
            q = early + t * per + j

            @pl.when(q < pairs)
            def _():
                intra(q)

    loop(ticks, tick)

    ones_row = lax.broadcasted_iota(jnp.int32, (toks, LANES), 0) == toks - 1

    def inter(q):
        tail, head = weighted(q)
        x = x_ref[:, cols(q)]
        sh, sl = parts(ent[0, q])
        gh, gl = parts(ent[1, q])
        eg = head * g_ref[:, cols(q)]
        tx = tail * x
        s_wide = jnp.concatenate([sh, sl], axis=1)
        g_wide = jnp.concatenate([gh, gl], axis=1)
        y = dot(cwide[...], jnp.concatenate([s_wide, s_wide], axis=0))
        y = y[:, :LANES] + y[:, LANES:]
        dxi = dot(bwide[...], jnp.concatenate([g_wide, g_wide], axis=0))
        dxi = tail * (dxi[:, :LANES] + dxi[:, LANES:])
        dx_ref[:, cols(q)] += dxi
        s_tall = jnp.concatenate([sh, sl], axis=0)
        g_tall = jnp.concatenate([gh, gl], axis=0)
        dc = dot(jnp.concatenate(parts(eg), axis=1), jnp.concatenate([s_tall, s_tall], axis=1), NT)
        bc[1] += dc[:, :LANES] + dc[:, LANES:]
        db = dot(jnp.concatenate(parts(tx), axis=1), jnp.concatenate([g_tall, g_tall], axis=1), NT)
        bc[0] += db[:, :LANES] + db[:, LANES:]
        across = jnp.sum(ent[0, q] * ent[1, q], axis=0, keepdims=True) * dec[pl.ds(q, 1), :]
        read = eg * y
        read = read + jnp.where(ones_row, across, 0.0)
        wrote = x * dxi
        for n in range(2):
            mask = low_left if n == 0 else jnp.logical_not(low_left)
            here = lane == 2 * q + n
            col_acc[...] += jnp.where(here, jnp.sum(jnp.where(mask, read, 0.0), axis=1, keepdims=True), 0.0)
            colq_acc[...] += jnp.where(here, jnp.sum(jnp.where(mask, wrote, 0.0), axis=1, keepdims=True), 0.0)

    if four:
        def side_in(k):
            inter(half0 + mine0 + k)
            for d in range(2):
                down1(d, k).wait_recv()
                finish_core(d, (1 - side) * qp + k)

        loop(qp, side_in)
        loop(qp, lambda k: inter(half0 + (1 - side) * qp + k))
    else:
        loop(hp, lambda k: inter(half0 + k))

    if two:
        def core_in(k):
            for d in range(2):
                down0(d, k).wait_recv()
            inter((1 - core) * hp + k)

        if four:
            loop(qp, lambda k: core_in(mine0 + k))
            loop(qp, lambda k: core_in((1 - side) * qp + k))
        else:
            loop(hp, core_in)

    dsh, dsl = parts(dscore[...])
    bc[0] += dot(dsh, c_high) + dot(dsh, c_low) + dot(dsl, c_high)
    bc[1] += dot(dsh, b_high, TN) + dot(dsh, b_low, TN) + dot(dsl, b_high, TN)
    for step in range(1, tp):
        tp_copy(step).start()

    later = (row_i >= col_i).astype(BF16)
    earlier = (row_i < col_i).astype(BF16)
    grad = exact_dot(col_acc[...], later, TN) + exact_dot(colq_acc[...], earlier, TN)
    da_ref[...] = grad[:heads] + exact_dot(rows_acc[0:heads, :], later, NN)

    own_rows = pl.ds(pl.multiple_of(my_tp * rt, rt), rt)
    db_sum = bc[0, own_rows]
    dc_sum = bc[1, own_rows]
    for step in range(1, tp):
        tp_copy(step).wait_recv()
        db_sum = db_sum + rtp[step - 1, 0]
        dc_sum = dc_sum + rtp[step - 1, 1]
    db_ref[...] = db_sum
    dc_ref[...] = dc_sum

    for step in range(1, tp):
        tp_copy(step).wait_send()

    def left(k):
        for d in range(2):
            has_after = place < groups - 1 if d == 0 else place > 0
            if four:
                up1(d, k).wait_send()
                down1(d, k).wait_send()

            @pl.when(has_after)
            def _():
                chain(d, k).wait_send()

    loop(qp, left)
    if two:
        def left_core(k):
            for d in range(2):
                down0(d, k).wait_send()

        loop(hp, left_core)


def per_device(ctx, tp, x, b, c, codes, g):
    heads, toks = codes.shape
    pairs = x.shape[1] // LANES
    hp = pairs // 2 if pairs % 2 == 0 else pairs
    qp = pairs // 4 if pairs % 4 == 0 else hp
    pad = -(-pairs // 8) * 8
    state = (LANES, LANES)
    copies = 4 + 6 * qp + 2 * hp + tp - 1
    vmem = pl.BlockSpec(memory_space=pltpu.VMEM)
    shape = jax.ShapeDtypeStruct
    return pl.pallas_call(
        functools.partial(kernel, ctx, tp),
        out_shape=(
            shape(x.shape, F32), shape((toks // tp, LANES), F32),
            shape((toks // tp, LANES), F32), shape(codes.shape, F32),
        ),
        in_specs=[vmem] * 5,
        out_specs=(vmem,) * 4,
        scratch_shapes=[
            pltpu.VMEM(x.shape, F32),
            pltpu.VMEM((2, pairs) + state, F32),
            pltpu.VMEM((pad, LANES), F32),
            pltpu.VMEM((pad, LANES), F32),
            pltpu.VMEM((pad, LANES), F32),
            pltpu.VMEM((pad, LANES), F32),
            pltpu.VMEM((2, hp) + state, F32),
            pltpu.VMEM((2, hp) + state, F32),
            pltpu.VMEM((2, qp) + state, F32),
            pltpu.VMEM((2, qp) + state, F32),
            pltpu.VMEM((2, qp) + state, F32),
            pltpu.VMEM((2, hp) + state, F32),
            pltpu.VMEM((2, qp) + state, F32),
            pltpu.VMEM((2, hp) + state, F32),
            pltpu.VMEM((2, pairs) + state, F32),
            pltpu.VMEM((toks, toks), F32),
            pltpu.VMEM((toks, toks), F32),
            pltpu.VMEM((-(-heads // 8) * 8, toks), F32),
            pltpu.VMEM((toks, LANES), F32),
            pltpu.VMEM((toks, LANES), F32),
            pltpu.VMEM((2, toks, LANES), F32),
            pltpu.VMEM((max(tp - 1, 1), 2, toks // tp, LANES), F32),
            pltpu.VMEM((toks, 2 * LANES), BF16),
            pltpu.VMEM((toks, 2 * LANES), BF16),
            pltpu.SemaphoreType.DMA((copies,)),
            pltpu.SemaphoreType.DMA((copies,)),
        ],
        compiler_params=pltpu.CompilerParams(
            collective_id=0, has_side_effects=True, vmem_limit_bytes=50 * 1024 * 1024
        ),
    )(x, b, c, codes, g)


def solution(mesh):
    placed = (P("ctx", "tp"), P("ctx", None), P("ctx", None), P("tp", "ctx"), P("ctx", "tp"))
    return jax.shard_map(
        functools.partial(per_device, mesh.shape["ctx"], mesh.shape["tp"]),
        mesh=mesh,
        in_specs=placed,
        out_specs=(P("ctx", "tp"), P(("ctx", "tp"), None), P(("ctx", "tp"), None), P("tp", "ctx")),
        check_vma=False,
    )
```

```python
import functools

import jax
import jax.numpy as jnp
from jax import lax
from jax.experimental import pallas as pl
from jax.experimental.pallas import tpu as pltpu
from jax.sharding import PartitionSpec as P

MESH = pl.DeviceIdType.MESH
CODE_UNIT = 2.0 ** (-16)
LANES = 128
HALF = 64
F32 = jnp.float32
BF16 = jnp.bfloat16
NN = (((1,), (0,)), ((), ()))
NT = (((1,), (1,)), ((), ()))
TN = (((0,), (0,)), ((), ()))


def dot(a, b, dims=NN):
    return lax.dot_general(a, b, dims, preferred_element_type=F32)


def parts(a):
    high = a.astype(BF16)
    return high, (a - high.astype(F32)).astype(BF16)


def exact_dot(a, ones, dims):
    first = a.astype(BF16)
    rest = a - first.astype(F32)
    second = rest.astype(BF16)
    third = (rest - second.astype(F32)).astype(BF16)
    return dot(first, ones, dims) + dot(second, ones, dims) + dot(third, ones, dims)


def swap(a):
    return pltpu.roll(a, HALF, 1)


def kernel(
    ctx, tp, x_hbm, b_hbm, c_hbm, code_hbm, g_hbm,
    dx_ref, db_ref, dc_ref, da_ref,
    wl, loc, dec, rdec0, dec1, rdec1, rbuf0, agg, rbuf1, zin, zout, zp, snd1, snd0, ent,
    score, dscore, rows_acc, col_acc, colq_acc, bc, rtp,
    cwide, bwide, x_ref, g_ref, b_ref, c_ref, code_ref, send, recv, fetched,
):
    heads, toks = code_ref.shape
    pairs = x_ref.shape[1] // LANES
    two = pairs % 2 == 0
    four = pairs % 4 == 0
    hp = pairs // 2 if two else pairs
    qp = pairs // 4 if four else hp
    group = 4 if four else 2 if two else 1
    groups = ctx // group
    mid = toks // 2

    me = lax.axis_index("ctx")
    my_tp = lax.axis_index("tp")
    place = me // group
    core = me % 2 if two else 0
    side = (me // 2) % 2 if four else 0
    core_mate = me + 1 - 2 * (me % 2)
    side_mate = me + 2 - 4 * ((me // 2) % 2)
    half0 = core * hp if two else 0
    mine0 = side * qp if four else 0

    if four:
        starts = [h * hp + s * qp for s in (1 - side, side) for h in (1 - core, core)]
    elif two:
        starts = [(1 - core) * hp, core * hp]
    else:
        starts = [0]

    def fetch(number):
        if number < 3:
            src, dst = ((code_hbm, code_ref), (b_hbm, b_ref), (c_hbm, c_ref))[number]
            return pltpu.make_async_copy(src, dst, fetched.at[number])
        part, which = (number - 3) // 2, (number - 3) % 2
        src, dst = ((x_hbm, x_ref), (g_hbm, g_ref))[which]
        span = pl.ds(pl.multiple_of(starts[part] * LANES, LANES), qp * LANES)
        return pltpu.make_async_copy(src.at[:, span], dst.at[:, span], fetched.at[number])

    def arrived(*which):
        for part in which:
            fetch(3 + 2 * part).wait()
            fetch(4 + 2 * part).wait()

    for number in range(3 + 2 * len(starts)):
        fetch(number).start()

    n_dec0 = 0
    n_dec1 = 1
    n_first = 2
    n_up = n_first + 2 * hp
    n_chain = n_up + 2 * qp
    n_down = n_chain + 2 * qp
    n_last = n_down + 2 * qp
    n_tp = n_last + 2 * hp

    def copy(src, dst, number, to):
        return pltpu.make_async_remote_copy(
            src_ref=src, dst_ref=dst, send_sem=send.at[number], recv_sem=recv.at[number],
            device_id=to, device_id_type=MESH,
        )

    def up0(d, k):
        return copy(
            loc.at[d, (1 - core) * hp + k], rbuf0.at[d, k], n_first + d * hp + k,
            {"ctx": core_mate},
        )

    def dec0_copy():
        return copy(dec, rdec0, n_dec0, {"ctx": core_mate})

    def dec1_copy():
        return copy(dec1, rdec1, n_dec1, {"ctx": side_mate})

    def up1(d, k):
        return copy(
            agg.at[d, k], rbuf1.at[d, k], n_up + d * qp + k, {"ctx": side_mate}
        )

    def chain(d, k):
        to = me + group if d == 0 else me - group
        return copy(zout.at[d, k], zin.at[d, k], n_chain + d * qp + k, {"ctx": to})

    def down1(d, k):
        return copy(
            snd1.at[d, k], zp.at[d, mine0 + k], n_down + d * qp + k, {"ctx": side_mate}
        )

    def down0(d, k):
        return copy(
            snd0.at[d, k], ent.at[d, half0 + k], n_last + d * hp + k, {"ctx": core_mate}
        )

    rt = toks // tp

    def tp_copy(step):
        to = lax.rem(my_tp + step, tp)
        return copy(
            bc.at[:, pl.ds(pl.multiple_of(to * rt, rt), rt)], rtp.at[step - 1],
            n_tp + step - 1, {"tp": to},
        )

    barrier = pltpu.get_barrier_semaphore()

    def greet(to):
        pl.semaphore_signal(barrier, inc=1, device_id=to, device_id_type=MESH)

    expected = tp - 1
    if two:
        greet({"ctx": core_mate})
        expected = expected + 1
    if four:
        greet({"ctx": side_mate})
        expected = expected + 1
    for step in range(1, tp):
        greet({"tp": lax.rem(my_tp + step, tp)})

    @pl.when(place > 0)
    def _():
        greet({"ctx": me - group})

    @pl.when(place < groups - 1)
    def _():
        greet({"ctx": me + group})

    inner = jnp.where(place > 0, 1, 0) + jnp.where(place < groups - 1, 1, 0)

    row_i = lax.broadcasted_iota(jnp.int32, (toks, toks), 0)
    col_i = lax.broadcasted_iota(jnp.int32, (toks, toks), 1)
    low_left = lax.broadcasted_iota(jnp.int32, (toks, LANES), 1) < HALF
    left_mid = lax.broadcasted_iota(jnp.int32, (mid, LANES), 1) < HALF
    lane = lax.broadcasted_iota(jnp.int32, (toks, LANES), 1)

    def cols(q):
        return pl.ds(pl.multiple_of(q * LANES, LANES), LANES)

    fetch(0).wait()
    codes = code_ref[...]
    code_high = lax.shift_right_logical(codes, 8).astype(F32)
    code_low = (codes & 255).astype(F32)
    upto = (col_i <= row_i).astype(BF16)
    run_high = dot(upto, code_high.astype(BF16), NT)
    run_low = dot(upto, code_low.astype(BF16), NT)
    total = run_high * 256.0 + run_low
    within_col = total * (-CODE_UNIT)

    rows_acc[...] = jnp.zeros_like(rows_acc)
    rows_acc[0:heads, :] = (
        dot(code_high.astype(BF16), (row_i <= col_i).astype(BF16)) * 256.0
        + dot(code_low.astype(BF16), (row_i <= col_i).astype(BF16))
    ) * (-CODE_UNIT)
    for q in range(pairs):
        wl[:, q * LANES:(q + 1) * LANES] = jnp.where(
            low_left, within_col[:, 2 * q:2 * q + 1], within_col[:, 2 * q + 1:2 * q + 2]
        )
    dec[...] = jnp.zeros_like(dec)
    for q in range(pairs):
        dec[q:q + 1, :] = jnp.exp(wl[toks - 1:toks, q * LANES:(q + 1) * LANES])

    fetch(1).wait()
    fetch(2).wait()
    b_high, b_low = parts(b_ref[...])
    c_high, c_low = parts(c_ref[...])
    bwide[...] = jnp.concatenate([b_high, b_low], axis=1)
    cwide[...] = jnp.concatenate([c_high, c_low], axis=1)
    b_tall = jnp.transpose(jnp.concatenate([b_high.astype(F32), b_low.astype(F32)], axis=1)).astype(BF16)
    c_tall = jnp.transpose(jnp.concatenate([c_high.astype(F32), c_low.astype(F32)], axis=1)).astype(BF16)

    def weighted(q):
        w = wl[:, cols(q)]
        tail = jnp.exp(wl[pl.ds(toks - 1, 1), cols(q)] - w)
        return tail, jnp.exp(w)

    def local_state(q):
        tail, head = weighted(q)
        for d, (tall, value) in enumerate(
            ((b_tall, tail * x_ref[:, cols(q)]), (c_tall, head * g_ref[:, cols(q)]))
        ):
            high, low = parts(value)
            out = dot(tall, jnp.concatenate([high, low], axis=1))
            out = out[:LANES] + out[LANES:]
            loc[d, q] = out[:, :LANES] + out[:, LANES:]

    def loop(count, body):
        lax.fori_loop(0, count, lambda k, _: (body(k), 0)[1], 0)

    pl.semaphore_wait(barrier, expected + inner)

    def make(k):
        local_state((1 - core) * hp + k)
        for d in range(2):
            up0(d, k).start()
        local_state(half0 + k)

    def join(d, k):
        own_first = core == d
        q = half0 + k
        one = jnp.ones((1, LANES), F32)
        mine, other = dec[pl.ds(q, 1), :], rdec0[pl.ds(q, 1), :]
        up0(d, k).wait_recv()
        return (
            jnp.where(own_first, other, one) * loc[d, q]
            + jnp.where(own_first, one, mine) * rbuf0[d, k]
        )

    def pass_up(k):
        for d in range(2):
            agg[d, k] = join(d, (1 - side) * qp + k)
            up1(d, k).start()

    if two:
        dec0_copy().start()
        arrived(0, 1)
        other0 = (1 - side) * qp if four else 0
        make(other0)
        dec0_copy().wait()
        dec1[...] = dec[...] * rdec0[...]
        if four:
            dec1_copy().start()

            def step_up(k):
                make(other0 + k + 1)
                pass_up(k)

            loop(qp - 1, step_up)
            pass_up(qp - 1)
            arrived(2, 3)
            loop(qp, lambda k: make(mine0 + k))
        else:
            loop(qp - 1, lambda k: make(k + 1))
    else:
        arrived(0)
        loop(pairs, local_state)
        dec1[...] = dec[...]

    score[...] = (
        dot(b_high, c_high, NT) + dot(b_high, c_low, NT) + dot(b_low, c_high, NT)
    )
    dscore[...] = jnp.zeros_like(dscore)
    col_acc[...] = jnp.zeros_like(col_acc)
    colq_acc[...] = jnp.zeros_like(colq_acc)
    bc[...] = jnp.zeros_like(bc)
    dx_ref[...] = jnp.zeros_like(dx_ref)
    causal = row_i <= col_i

    def intra(q):
        x = x_ref[:, cols(q)]
        g = g_ref[:, cols(q)]
        w = wl[:, cols(q)]
        xh = x.astype(BF16).astype(F32)
        xl = x - xh
        gh = g.astype(BF16).astype(F32)
        gl = g - gh
        xl_s, gh_s, gl_s, w_s = swap(xl), swap(gh), swap(gl), swap(w)
        xh_b, gh_b = xh.astype(BF16), gh.astype(BF16)
        zero = jnp.zeros_like(g)
        results = []
        for n in range(2):
            if n == 0:
                pick = lambda a, b: jnp.where(low_left, a, b)
            else:
                pick = lambda a, b: jnp.where(low_left, b, a)
            left = jnp.concatenate([pick(xh, xl_s).astype(BF16), xh_b], axis=1)
            right = jnp.concatenate([pick(gh, gh_s).astype(BF16), pick(gl, zero).astype(BF16)], axis=1)
            value = pick(gh, gl_s).astype(BF16)
            w_here = pick(w, w_s)
            row = rows_acc[pl.ds(2 * q + n, 1), :]
            out = []
            colsum = []
            rowsum = []
            for r in range(2):
                here = slice(r * mid, (r + 1) * mid)
                after = slice(r * mid, toks)
                width = toks - r * mid
                wh = w_here[here]
                wide = jnp.concatenate([wh] * (width // LANES), axis=1)
                gap = jnp.where(causal[here, after], row[:, after] - wide, -1e30)
                decay = jnp.exp(gap)
                dm = dot(left[here], right[after], NT)
                scaled = dm * decay
                sc = score[here, after]
                dscore[here, after] += scaled
                z = scaled * sc
                colsum.append(jnp.sum(z, axis=0, keepdims=True))
                rowsum.append(jnp.sum(z, axis=1, keepdims=True))
                mh, ml = parts(decay * sc)
                main = dot(mh, value[after])
                out.append(main + swap(main) + dot(ml, gh_b[after]))
            results.append(jnp.concatenate(out, axis=0))
            rows_acc[pl.ds(2 * q + n, 1), :] = jnp.concatenate(
                [colsum[0][:, :mid], colsum[0][:, mid:] + colsum[1]], axis=1
            )
            col_acc[...] -= jnp.where(lane == 2 * q + n, jnp.concatenate(rowsum, axis=0), 0.0)
        dx_ref[:, cols(q)] += jnp.where(low_left, results[0], results[1])

    early = pairs // 4
    loop(early, intra)
    if four:
        dec1_copy().wait()

    def finish_core(d, k):
        q = half0 + k
        z = zp[d, k]
        if not two:
            ent[d, q] = z
            return
        own_first = core == d
        first_dec = jnp.where(own_first, dec[pl.ds(q, 1), :], rdec0[pl.ds(q, 1), :])
        first = jnp.where(own_first, loc[d, q], rbuf0[d, k])
        later = first_dec * z + first
        ent[d, q] = jnp.where(own_first, z, later)
        snd0[d, k] = jnp.where(own_first, later, z)
        down0(d, k).start()

    def carry(d, k):
        q = half0 + mine0 + k
        has_before = place > 0 if d == 0 else place < groups - 1
        has_after = place < groups - 1 if d == 0 else place > 0
        own = join(d, mine0 + k) if two else loc[d, k]
        mine = dec1[pl.ds(q, 1), :]
        if four:
            up1(d, k).wait_recv()
            other = rdec1[pl.ds(q, 1), :]
            got = rbuf1[d, k]
            own_first = side == d
            one = jnp.ones((1, LANES), F32)
            full = jnp.where(own_first, other, one) * own + jnp.where(own_first, one, mine) * got
            full_dec = mine * other
        else:
            full, full_dec = own, mine

        @pl.when(has_before)
        def _():
            chain(d, k).wait_recv()

        @pl.when(jnp.logical_not(has_before))
        def _():
            zin[d, k] = jnp.zeros((LANES, LANES), F32)

        z = zin[d, k]

        @pl.when(has_after)
        def _():
            zout[d, k] = full_dec * z + full
            chain(d, k).start()

        if four:
            first_dec = jnp.where(own_first, mine, other)
            later = first_dec * z + jnp.where(own_first, own, got)
            snd1[d, k] = jnp.where(own_first, later, z)
            down1(d, k).start()
            zp[d, mine0 + k] = jnp.where(own_first, z, later)
        else:
            zp[d, mine0 + k] = z
        finish_core(d, mine0 + k)

    ones_row = lax.broadcasted_iota(jnp.int32, (toks, LANES), 0) == toks - 1

    def inter(q):
        tail, head = weighted(q)
        x = x_ref[:, cols(q)]
        sh, sl = parts(ent[0, q])
        gh, gl = parts(ent[1, q])
        eg = head * g_ref[:, cols(q)]
        tx = tail * x
        s_wide = jnp.concatenate([sh, sl], axis=1)
        g_wide = jnp.concatenate([gh, gl], axis=1)
        y = dot(cwide[...], jnp.concatenate([s_wide, s_wide], axis=0))
        y = y[:, :LANES] + y[:, LANES:]
        dxi = dot(bwide[...], jnp.concatenate([g_wide, g_wide], axis=0))
        dxi = tail * (dxi[:, :LANES] + dxi[:, LANES:])
        dx_ref[:, cols(q)] += dxi
        s_tall = jnp.concatenate([sh, sl], axis=0)
        g_tall = jnp.concatenate([gh, gl], axis=0)
        dc = dot(jnp.concatenate(parts(eg), axis=1), jnp.concatenate([s_tall, s_tall], axis=1), NT)
        bc[1] += dc[:, :LANES] + dc[:, LANES:]
        db = dot(jnp.concatenate(parts(tx), axis=1), jnp.concatenate([g_tall, g_tall], axis=1), NT)
        bc[0] += db[:, :LANES] + db[:, LANES:]
        across = jnp.sum(ent[0, q] * ent[1, q], axis=0, keepdims=True) * dec[pl.ds(q, 1), :]
        read = eg * y
        read = read + jnp.where(ones_row, across, 0.0)
        wrote = x * dxi
        for n in range(2):
            mask = low_left if n == 0 else jnp.logical_not(low_left)
            here = lane == 2 * q + n
            col_acc[...] += jnp.where(here, jnp.sum(jnp.where(mask, read, 0.0), axis=1, keepdims=True), 0.0)
            colq_acc[...] += jnp.where(here, jnp.sum(jnp.where(mask, wrote, 0.0), axis=1, keepdims=True), 0.0)

    both = jnp.maximum(place, groups - 1 - place)
    lag = 2 if four else 1 if two else 0
    intra_ticks = groups + 1
    per = -(-(pairs - early) // intra_ticks)

    def tick(t):
        def when_in(k, body):
            @pl.when(jnp.logical_and(k >= 0, k < qp))
            def _():
                body(k)

        for d in range(2):
            when_in(t - (place if d == 0 else groups - 1 - place), functools.partial(carry, d))
        now = t - both

        def side_in(k):
            for d in range(2):
                down1(d, k).wait_recv()
                finish_core(d, (1 - side) * qp + k)

        def core_in(k):
            for d in range(2):
                down0(d, k).wait_recv()
            inter((1 - core) * hp + k)

        if four:
            when_in(now - 1, side_in)
        for j in range(per):
            q = early + t * per + j

            @pl.when(q < pairs)
            def _():
                intra(q)

        when_in(now, lambda k: inter(half0 + mine0 + k))
        if four:
            when_in(now - 1, lambda k: inter(half0 + (1 - side) * qp + k))
        if two:
            when_in(now - 1, lambda k: core_in(mine0 + k))
        if four:
            when_in(now - 2, lambda k: core_in((1 - side) * qp + k))

    loop(groups - 1 + qp + lag, tick)

    dsh, dsl = parts(dscore[...])
    bc[0] += dot(dsh, c_high) + dot(dsh, c_low) + dot(dsl, c_high)
    bc[1] += dot(dsh, b_high, TN) + dot(dsh, b_low, TN) + dot(dsl, b_high, TN)
    for step in range(1, tp):
        tp_copy(step).start()

    later = (row_i >= col_i).astype(BF16)
    earlier = (row_i < col_i).astype(BF16)
    grad = exact_dot(col_acc[...], later, TN) + exact_dot(colq_acc[...], earlier, TN)
    da_ref[...] = grad[:heads] + exact_dot(rows_acc[0:heads, :], later, NN)

    own_rows = pl.ds(pl.multiple_of(my_tp * rt, rt), rt)
    db_sum = bc[0, own_rows]
    dc_sum = bc[1, own_rows]
    for step in range(1, tp):
        tp_copy(step).wait_recv()
        db_sum = db_sum + rtp[step - 1, 0]
        dc_sum = dc_sum + rtp[step - 1, 1]
    db_ref[...] = db_sum
    dc_ref[...] = dc_sum

    for step in range(1, tp):
        tp_copy(step).wait_send()

    def left(k):
        for d in range(2):
            has_after = place < groups - 1 if d == 0 else place > 0
            if four:
                up1(d, k).wait_send()
                down1(d, k).wait_send()

            @pl.when(has_after)
            def _():
                chain(d, k).wait_send()

    loop(qp, left)
    if two:
        def left_core(k):
            for d in range(2):
                up0(d, k).wait_send()
                down0(d, k).wait_send()

        loop(hp, left_core)


def store(*refs):
    done = refs[-1]
    half = (len(refs) - 1) // 2
    copies = [
        pltpu.make_async_copy(refs[n], refs[half + n], done.at[n]) for n in range(half)
    ]
    for one in copies:
        one.start()
    for one in copies:
        one.wait()


def per_device(ctx, tp, x, b, c, codes, g):
    heads, toks = codes.shape
    pairs = x.shape[1] // LANES
    hp = pairs // 2 if pairs % 2 == 0 else pairs
    qp = pairs // 4 if pairs % 4 == 0 else hp
    pad = -(-pairs // 8) * 8
    state = (LANES, LANES)
    copies = 2 + 6 * qp + 4 * hp + tp - 1
    vmem = pl.BlockSpec(memory_space=pltpu.VMEM)
    shape = jax.ShapeDtypeStruct
    outs = pl.pallas_call(
        functools.partial(kernel, ctx, tp),
        out_shape=(
            shape(x.shape, F32), shape((toks // tp, LANES), F32),
            shape((toks // tp, LANES), F32), shape(codes.shape, F32),
        ),
        in_specs=[pl.BlockSpec(memory_space=pltpu.HBM)] * 5,
        out_specs=(vmem,) * 4,
        scratch_shapes=[
            pltpu.VMEM(x.shape, F32),
            pltpu.VMEM((2, pairs) + state, F32),
            pltpu.VMEM((pad, LANES), F32),
            pltpu.VMEM((pad, LANES), F32),
            pltpu.VMEM((pad, LANES), F32),
            pltpu.VMEM((pad, LANES), F32),
            pltpu.VMEM((2, hp) + state, F32),
            pltpu.VMEM((2, qp) + state, F32),
            pltpu.VMEM((2, qp) + state, F32),
            pltpu.VMEM((2, qp) + state, F32),
            pltpu.VMEM((2, qp) + state, F32),
            pltpu.VMEM((2, hp) + state, F32),
            pltpu.VMEM((2, qp) + state, F32),
            pltpu.VMEM((2, hp) + state, F32),
            pltpu.VMEM((2, pairs) + state, F32),
            pltpu.VMEM((toks, toks), F32),
            pltpu.VMEM((toks, toks), F32),
            pltpu.VMEM((-(-heads // 8) * 8, toks), F32),
            pltpu.VMEM((toks, LANES), F32),
            pltpu.VMEM((toks, LANES), F32),
            pltpu.VMEM((2, toks, LANES), F32),
            pltpu.VMEM((max(tp - 1, 1), 2, toks // tp, LANES), F32),
            pltpu.VMEM((toks, 2 * LANES), BF16),
            pltpu.VMEM((toks, 2 * LANES), BF16),
            pltpu.VMEM(x.shape, F32),
            pltpu.VMEM(x.shape, F32),
            pltpu.VMEM(b.shape, F32),
            pltpu.VMEM(c.shape, F32),
            pltpu.VMEM(codes.shape, jnp.int32),
            pltpu.SemaphoreType.DMA((copies,)),
            pltpu.SemaphoreType.DMA((copies,)),
            pltpu.SemaphoreType.DMA((11,)),
        ],
        compiler_params=pltpu.CompilerParams(
            collective_id=0, has_side_effects=True, vmem_limit_bytes=50 * 1024 * 1024
        ),
    )(x, b, c, codes, g)
    return pl.pallas_call(
        store,
        out_shape=tuple(shape(one.shape, F32) for one in outs),
        in_specs=[vmem] * 4,
        out_specs=(pl.BlockSpec(memory_space=pltpu.HBM),) * 4,
        scratch_shapes=[pltpu.SemaphoreType.DMA((4,))],
        compiler_params=pltpu.CompilerParams(vmem_limit_bytes=8 * 1024 * 1024),
    )(*outs)


def solution(mesh):
    placed = (P("ctx", "tp"), P("ctx", None), P("ctx", None), P("tp", "ctx"), P("ctx", "tp"))
    return jax.shard_map(
        functools.partial(per_device, mesh.shape["ctx"], mesh.shape["tp"]),
        mesh=mesh,
        in_specs=placed,
        out_specs=(P("ctx", "tp"), P(("ctx", "tp"), None), P(("ctx", "tp"), None), P("tp", "ctx")),
        check_vma=False,
    )
```

```python
import functools

import jax
import jax.numpy as jnp
from jax import lax
from jax.experimental import pallas as pl
from jax.experimental.pallas import tpu as pltpu
from jax.sharding import PartitionSpec as P

MESH = pl.DeviceIdType.MESH
CODE_UNIT = 2.0 ** (-16)
LANES = 128
HALF = 64
F32 = jnp.float32
BF16 = jnp.bfloat16
NN = (((1,), (0,)), ((), ()))
NT = (((1,), (1,)), ((), ()))
TN = (((0,), (0,)), ((), ()))


def dot(a, b, dims=NN):
    return lax.dot_general(a, b, dims, preferred_element_type=F32)


def parts(a):
    high = a.astype(BF16)
    return high, (a - high.astype(F32)).astype(BF16)


def exact_dot(a, ones, dims):
    first = a.astype(BF16)
    rest = a - first.astype(F32)
    second = rest.astype(BF16)
    third = (rest - second.astype(F32)).astype(BF16)
    return dot(first, ones, dims) + dot(second, ones, dims) + dot(third, ones, dims)


def swap(a):
    return pltpu.roll(a, HALF, 1)


def kernel(
    ctx, tp, x_hbm, g_hbm, small_ref,
    dx_ref, db_ref, dc_ref, da_ref,
    wl, loc, dec, rdec0, dec1, rdec1, rbuf0, agg, rbuf1, zin, zout, zp, snd1, snd0, ent,
    score, dscore, w_rows, rows_acc, rowsq_acc, bc, rtp,
    cwide, bwide, wides, x_ref, g_ref, send, recv, fetched,
):
    heads, toks = da_ref.shape
    pairs = x_ref.shape[1] // LANES
    two = pairs % 2 == 0
    four = pairs % 4 == 0
    hp = pairs // 2 if two else pairs
    qp = pairs // 4 if four else hp
    group = 4 if four else 2 if two else 1
    groups = ctx // group
    mid = toks // 2

    me = lax.axis_index("ctx")
    my_tp = lax.axis_index("tp")
    place = me // group
    core = me % 2 if two else 0
    side = (me // 2) % 2 if four else 0
    core_mate = me + 1 - 2 * (me % 2)
    side_mate = me + 2 - 4 * ((me // 2) % 2)
    half0 = core * hp if two else 0
    mine0 = side * qp if four else 0

    if four:
        starts = [h * hp + s * qp for s in (1 - side, side) for h in (1 - core, core)]
    elif two:
        starts = [(1 - core) * hp, core * hp]
    else:
        starts = [0]

    def fetch(number):
        part, which = number // 2, number % 2
        src, dst = ((x_hbm, x_ref), (g_hbm, g_ref))[which]
        span = pl.ds(pl.multiple_of(starts[part] * LANES, LANES), qp * LANES)
        return pltpu.make_async_copy(src.at[:, span], dst.at[:, span], fetched.at[number])

    def arrived(*which):
        for part in which:
            fetch(2 * part).wait()
            fetch(2 * part + 1).wait()

    for number in range(2 * len(starts)):
        fetch(number).start()

    n_dec0 = 0
    n_dec1 = 1
    n_first = 2
    n_up = n_first + 2 * hp
    n_chain = n_up + 2 * qp
    n_down = n_chain + 2 * qp
    n_last = n_down + 2 * qp
    n_tp = n_last + 2 * hp

    def copy(src, dst, number, to):
        return pltpu.make_async_remote_copy(
            src_ref=src, dst_ref=dst, send_sem=send.at[number], recv_sem=recv.at[number],
            device_id=to, device_id_type=MESH,
        )

    def up0(d, k):
        return copy(
            loc.at[d, (1 - core) * hp + k], rbuf0.at[d, k], n_first + d * hp + k,
            {"ctx": core_mate},
        )

    def dec0_copy():
        return copy(dec, rdec0, n_dec0, {"ctx": core_mate})

    def dec1_copy():
        return copy(dec1, rdec1, n_dec1, {"ctx": side_mate})

    def up1(d, k):
        return copy(
            agg.at[d, k], rbuf1.at[d, k], n_up + d * qp + k, {"ctx": side_mate}
        )

    def chain(d, k):
        to = me + group if d == 0 else me - group
        return copy(zout.at[d, k], zin.at[d, k], n_chain + d * qp + k, {"ctx": to})

    def down1(d, k):
        return copy(
            snd1.at[d, k], zp.at[d, mine0 + k], n_down + d * qp + k, {"ctx": side_mate}
        )

    def down0(d, k):
        return copy(
            snd0.at[d, k], ent.at[d, half0 + k], n_last + d * hp + k, {"ctx": core_mate}
        )

    rt = toks // tp

    def tp_copy(step):
        to = lax.rem(my_tp + step, tp)
        return copy(
            bc.at[:, pl.ds(pl.multiple_of(to * rt, rt), rt)], rtp.at[step - 1],
            n_tp + step - 1, {"tp": to},
        )

    barrier = pltpu.get_barrier_semaphore()

    def greet(to):
        pl.semaphore_signal(barrier, inc=1, device_id=to, device_id_type=MESH)

    expected = tp - 1
    if two:
        greet({"ctx": core_mate})
        expected = expected + 1
    if four:
        greet({"ctx": side_mate})
        expected = expected + 1
    for step in range(1, tp):
        greet({"tp": lax.rem(my_tp + step, tp)})

    @pl.when(place > 0)
    def _():
        greet({"ctx": me - group})

    @pl.when(place < groups - 1)
    def _():
        greet({"ctx": me + group})

    inner = jnp.where(place > 0, 1, 0) + jnp.where(place < groups - 1, 1, 0)

    row_i = lax.broadcasted_iota(jnp.int32, (toks, toks), 0)
    col_i = lax.broadcasted_iota(jnp.int32, (toks, toks), 1)
    low_left = lax.broadcasted_iota(jnp.int32, (toks, LANES), 1) < HALF

    def cols(q):
        return pl.ds(pl.multiple_of(q * LANES, LANES), LANES)

    codes = small_ref[toks:toks + heads, 0:toks]
    code_high = jnp.floor(codes * (1.0 / 256.0))
    code_low = codes - code_high * 256.0
    upto = (col_i <= row_i).astype(BF16)
    run_high = dot(upto, code_high.astype(BF16), NT)
    run_low = dot(upto, code_low.astype(BF16), NT)
    total = run_high * 256.0 + run_low
    within_col = total * (-CODE_UNIT)

    w_rows[...] = jnp.zeros_like(w_rows)
    rows_acc[...] = jnp.zeros_like(rows_acc)
    rowsq_acc[...] = jnp.zeros_like(rowsq_acc)
    w_rows[0:heads, :] = (
        dot(code_high.astype(BF16), (row_i <= col_i).astype(BF16)) * 256.0
        + dot(code_low.astype(BF16), (row_i <= col_i).astype(BF16))
    ) * (-CODE_UNIT)
    for q in range(pairs):
        wl[:, q * LANES:(q + 1) * LANES] = jnp.where(
            low_left, within_col[:, 2 * q:2 * q + 1], within_col[:, 2 * q + 1:2 * q + 2]
        )
    dec[...] = jnp.zeros_like(dec)
    for q in range(pairs):
        dec[q:q + 1, :] = jnp.exp(wl[toks - 1:toks, q * LANES:(q + 1) * LANES])

    b_high, b_low = parts(small_ref[0:toks, :LANES])
    c_high, c_low = parts(small_ref[0:toks, LANES:])
    bwide[...] = jnp.concatenate([b_high, b_low], axis=1)
    cwide[...] = jnp.concatenate([c_high, c_low], axis=1)
    b_tall = jnp.transpose(jnp.concatenate([b_high.astype(F32), b_low.astype(F32)], axis=1)).astype(BF16)
    c_tall = jnp.transpose(jnp.concatenate([c_high.astype(F32), c_low.astype(F32)], axis=1)).astype(BF16)

    def weighted(q):
        w = wl[:, cols(q)]
        tail = jnp.exp(wl[pl.ds(toks - 1, 1), cols(q)] - w)
        return tail, jnp.exp(w)

    def local_state(q):
        tail, head = weighted(q)
        for d, (tall, value) in enumerate(
            ((b_tall, tail * x_ref[:, cols(q)]), (c_tall, head * g_ref[:, cols(q)]))
        ):
            high, low = parts(value)
            wide = jnp.concatenate([high, low], axis=1)
            wides[d, q] = wide
            out = dot(tall, wide)
            out = out[:LANES] + out[LANES:]
            loc[d, q] = out[:, :LANES] + out[:, LANES:]

    def loop(count, body):
        lax.fori_loop(0, count, lambda k, _: (body(k), 0)[1], 0)

    pl.semaphore_wait(barrier, expected + inner)

    def make(k):
        local_state((1 - core) * hp + k)
        local_state(half0 + k)
        for d in range(2):
            up0(d, k).start()

    def join(d, k):
        own_first = core == d
        q = half0 + k
        one = jnp.ones((1, LANES), F32)
        mine, other = dec[pl.ds(q, 1), :], rdec0[pl.ds(q, 1), :]
        up0(d, k).wait_recv()
        return (
            jnp.where(own_first, other, one) * loc[d, q]
            + jnp.where(own_first, one, mine) * rbuf0[d, k]
        )

    def pass_up(k):
        for d in range(2):
            agg[d, k] = join(d, (1 - side) * qp + k)
            up1(d, k).start()

    if two:
        dec0_copy().start()
        arrived(0, 1)
        other0 = (1 - side) * qp if four else 0
        make(other0)
        dec0_copy().wait()
        dec1[...] = dec[...] * rdec0[...]
        if four:
            dec1_copy().start()

            def step_up(k):
                make(other0 + k + 1)
                pass_up(k)

            loop(qp - 1, step_up)
            pass_up(qp - 1)
            arrived(2, 3)
            loop(qp, lambda k: make(mine0 + k))
        else:
            loop(qp - 1, lambda k: make(k + 1))
    else:
        arrived(0)
        loop(pairs, local_state)
        dec1[...] = dec[...]

    score[...] = (
        dot(b_high, c_high, NT) + dot(b_high, c_low, NT) + dot(b_low, c_high, NT)
    )
    dscore[...] = jnp.zeros_like(dscore)
    bc[...] = jnp.zeros_like(bc)
    dx_ref[...] = jnp.zeros_like(dx_ref)
    causal = row_i <= col_i

    def head_rows(a):
        turned = jnp.transpose(a)
        return [jnp.sum(turned[n * HALF:(n + 1) * HALF], axis=0, keepdims=True) for n in range(2)]

    def intra(*pair_list):
        pair_rows = [[w_rows[pl.ds(2 * q + n, 1), :] for n in range(2)] for q in pair_list]
        finished = []
        for q, w_row in zip(pair_list, pair_rows):
            x = x_ref[:, cols(q)]
            g = g_ref[:, cols(q)]
            w = wl[:, cols(q)]
            xh = x.astype(BF16).astype(F32)
            xl = x - xh
            gh = g.astype(BF16).astype(F32)
            gl = g - gh
            xl_s, gh_s, gl_s, w_s = swap(xl), swap(gh), swap(gl), swap(w)
            xh_b, gh_b = xh.astype(BF16), gh.astype(BF16)
            zero = jnp.zeros_like(g)
            results, folded, colsums = [], [], []
            for n in range(2):
                if n == 0:
                    pick = lambda a, b: jnp.where(low_left, a, b)
                else:
                    pick = lambda a, b: jnp.where(low_left, b, a)
                left = jnp.concatenate([pick(xh, xl_s).astype(BF16), xh_b], axis=1)
                right = jnp.concatenate(
                    [pick(gh, gh_s).astype(BF16), pick(gl, zero).astype(BF16)], axis=1
                )
                value = pick(gh, gl_s).astype(BF16)
                w_here = pick(w, w_s)
                dm = dot(left, right, NT)
                high, low, fold, colsum = [], [], [], []
                for r in range(2):
                    here = slice(r * mid, (r + 1) * mid)
                    after = slice(r * mid, toks)
                    width = toks - r * mid
                    wide = jnp.concatenate([w_here[here]] * (width // LANES), axis=1)
                    gap = jnp.where(causal[here, after], w_row[n][:, after] - wide, -1e30)
                    decay = jnp.exp(gap)
                    scaled = dm[here, after] * decay
                    sc = score[here, after]
                    dscore[here, after] += scaled
                    z = scaled * sc
                    colsum.append(jnp.sum(z, axis=0, keepdims=True))
                    fold.append(sum(z[:, i * LANES:(i + 1) * LANES] for i in range(width // LANES)))
                    mh, ml = parts(decay * sc)
                    if r:
                        nothing = jnp.zeros((mid, mid), BF16)
                        mh = jnp.concatenate([nothing, mh], axis=1)
                        ml = jnp.concatenate([nothing, ml], axis=1)
                    high.append(mh)
                    low.append(ml)
                main = dot(jnp.concatenate(high, axis=0), value)
                results.append(main + swap(main) + dot(jnp.concatenate(low, axis=0), gh_b))
                fold = jnp.concatenate(fold, axis=0)
                folded.append(fold + swap(fold))
                colsums.append(
                    jnp.concatenate([colsum[0][:, :mid], colsum[0][:, mid:] + colsum[1]], axis=1)
                )
            rowsums = head_rows(jnp.where(low_left, folded[0], folded[1]))
            finished.append((
                jnp.where(low_left, results[0], results[1]),
                [colsums[n] - rowsums[n] for n in range(2)],
            ))
        for q, (dx, rows) in zip(pair_list, finished):
            dx_ref[:, cols(q)] += dx
            for n in range(2):
                rows_acc[pl.ds(2 * q + n, 1), :] += rows[n]

    early = pairs // 4
    loop(early // 2, lambda k: intra(2 * k, 2 * k + 1))
    if early % 2:
        intra(early - 1)
    if four:
        dec1_copy().wait()

    def finish_core(d, k):
        q = half0 + k
        z = zp[d, k]
        if not two:
            ent[d, q] = z
            return
        own_first = core == d
        first_dec = jnp.where(own_first, dec[pl.ds(q, 1), :], rdec0[pl.ds(q, 1), :])
        first = jnp.where(own_first, loc[d, q], rbuf0[d, k])
        later = first_dec * z + first
        ent[d, q] = jnp.where(own_first, z, later)
        snd0[d, k] = jnp.where(own_first, later, z)
        down0(d, k).start()

    def carry(d, k):
        q = half0 + mine0 + k
        has_before = place > 0 if d == 0 else place < groups - 1
        has_after = place < groups - 1 if d == 0 else place > 0
        own = join(d, mine0 + k) if two else loc[d, k]
        mine = dec1[pl.ds(q, 1), :]
        if four:
            up1(d, k).wait_recv()
            other = rdec1[pl.ds(q, 1), :]
            got = rbuf1[d, k]
            own_first = side == d
            one = jnp.ones((1, LANES), F32)
            full = jnp.where(own_first, other, one) * own + jnp.where(own_first, one, mine) * got
            full_dec = mine * other
        else:
            full, full_dec = own, mine

        @pl.when(has_before)
        def _():
            chain(d, k).wait_recv()

        @pl.when(jnp.logical_not(has_before))
        def _():
            zin[d, k] = jnp.zeros((LANES, LANES), F32)

        z = zin[d, k]

        @pl.when(has_after)
        def _():
            zout[d, k] = full_dec * z + full
            chain(d, k).start()

        if four:
            first_dec = jnp.where(own_first, mine, other)
            later = first_dec * z + jnp.where(own_first, own, got)
            snd1[d, k] = jnp.where(own_first, later, z)
            down1(d, k).start()
            zp[d, mine0 + k] = jnp.where(own_first, z, later)
        else:
            zp[d, mine0 + k] = z
        finish_core(d, mine0 + k)

    ones_row = lax.broadcasted_iota(jnp.int32, (toks, LANES), 0) == toks - 1

    def inter(*pair_list):
        db_sum, dc_sum = 0.0, 0.0
        finished = []
        for q in pair_list:
            tail = jnp.exp(wl[pl.ds(toks - 1, 1), cols(q)] - wl[:, cols(q)])
            sh, sl = parts(ent[0, q])
            gh, gl = parts(ent[1, q])
            tx, eg = wides[0, q], wides[1, q]
            s_wide = jnp.concatenate([sh, sl], axis=1)
            g_wide = jnp.concatenate([gh, gl], axis=1)
            y = dot(cwide[...], jnp.concatenate([s_wide, s_wide], axis=0))
            y = y[:, :LANES] + y[:, LANES:]
            dxi = dot(bwide[...], jnp.concatenate([g_wide, g_wide], axis=0))
            dxi = dxi[:, :LANES] + dxi[:, LANES:]
            s_tall = jnp.concatenate([sh, sl], axis=0)
            g_tall = jnp.concatenate([gh, gl], axis=0)
            dc_sum += dot(eg, jnp.concatenate([s_tall, s_tall], axis=1), NT)
            db_sum += dot(tx, jnp.concatenate([g_tall, g_tall], axis=1), NT)
            across = jnp.sum(ent[0, q] * ent[1, q], axis=0, keepdims=True) * dec[pl.ds(q, 1), :]
            read = (eg[:, :LANES].astype(F32) + eg[:, LANES:].astype(F32)) * y
            read = read + jnp.where(ones_row, across, 0.0)
            wrote = (tx[:, :LANES].astype(F32) + tx[:, LANES:].astype(F32)) * dxi
            finished.append((tail * dxi, head_rows(read), head_rows(wrote)))
        bc[0] += db_sum[:, :LANES] + db_sum[:, LANES:]
        bc[1] += dc_sum[:, :LANES] + dc_sum[:, LANES:]
        for q, (dx, rows, rowsq) in zip(pair_list, finished):
            dx_ref[:, cols(q)] += dx
            for n in range(2):
                rows_acc[pl.ds(2 * q + n, 1), :] += rows[n]
                rowsq_acc[pl.ds(2 * q + n, 1), :] = rowsq[n]

    both = jnp.maximum(place, groups - 1 - place)
    lag = 2 if four else 1 if two else 0
    intra_ticks = groups + 1
    per = -(-(pairs - early) // intra_ticks)

    def tick(t):
        def when_in(k, body):
            @pl.when(jnp.logical_and(k >= 0, k < qp))
            def _():
                body(k)

        for d in range(2):
            when_in(t - (place if d == 0 else groups - 1 - place), functools.partial(carry, d))
        now = t - both

        def side_in(k):
            for d in range(2):
                down1(d, k).wait_recv()
                finish_core(d, (1 - side) * qp + k)

        def core_wait(k):
            for d in range(2):
                down0(d, k).wait_recv()

        def first_three(k):
            core_wait(mine0 + k)
            inter(half0 + mine0 + k, half0 + (1 - side) * qp + k, (1 - core) * hp + mine0 + k)

        def last_one(k):
            core_wait((1 - side) * qp + k)
            inter((1 - core) * hp + (1 - side) * qp + k)

        def first_two(k):
            core_wait(k)
            inter(half0 + k, (1 - core) * hp + k)

        if four:
            when_in(now - 1, side_in)
        q0 = early + t * per
        if (pairs - early) % per == 0:
            @pl.when(q0 < pairs)
            def _():
                intra(*[q0 + j for j in range(per)])
        else:
            for j in range(per):
                @pl.when(q0 + j < pairs)
                def _():
                    intra(q0 + j)

        if four:
            when_in(now - 1, first_three)
            when_in(now - 2, last_one)
        elif two:
            when_in(now - 1, first_two)
        else:
            when_in(now, inter)

    loop(groups - 1 + qp + lag, tick)

    dsh, dsl = parts(dscore[...])
    bc[0] += dot(dsh, c_high) + dot(dsh, c_low) + dot(dsl, c_high)
    bc[1] += dot(dsh, b_high, TN) + dot(dsh, b_low, TN) + dot(dsl, b_high, TN)
    for step in range(1, tp):
        tp_copy(step).start()

    later = (row_i >= col_i).astype(BF16)
    earlier = (row_i < col_i).astype(BF16)
    da_ref[...] = exact_dot(rows_acc[0:heads, :], later, NN) + exact_dot(
        rowsq_acc[0:heads, :], earlier, NN
    )

    own_rows = pl.ds(pl.multiple_of(my_tp * rt, rt), rt)
    db_sum = bc[0, own_rows]
    dc_sum = bc[1, own_rows]
    for step in range(1, tp):
        tp_copy(step).wait_recv()
        db_sum = db_sum + rtp[step - 1, 0]
        dc_sum = dc_sum + rtp[step - 1, 1]
    db_ref[...] = db_sum
    dc_ref[...] = dc_sum

    for step in range(1, tp):
        tp_copy(step).wait_send()

    def left(k):
        for d in range(2):
            has_after = place < groups - 1 if d == 0 else place > 0
            if four:
                up1(d, k).wait_send()
                down1(d, k).wait_send()

            @pl.when(has_after)
            def _():
                chain(d, k).wait_send()

    loop(qp, left)
    if two:
        def left_core(k):
            for d in range(2):
                up0(d, k).wait_send()
                down0(d, k).wait_send()

        loop(hp, left_core)


def store(*refs):
    done = refs[-1]
    half = (len(refs) - 1) // 2
    copies = [
        pltpu.make_async_copy(refs[n], refs[half + n], done.at[n]) for n in range(half)
    ]
    for one in copies:
        one.start()
    for one in copies:
        one.wait()


def per_device(ctx, tp, x, b, c, codes, g):
    heads, toks = codes.shape
    pairs = x.shape[1] // LANES
    hp = pairs // 2 if pairs % 2 == 0 else pairs
    qp = pairs // 4 if pairs % 4 == 0 else hp
    pad = -(-pairs // 8) * 8
    state = (LANES, LANES)
    copies = 2 + 6 * qp + 4 * hp + tp - 1
    vmem = pl.BlockSpec(memory_space=pltpu.VMEM)
    shape = jax.ShapeDtypeStruct
    small = (
        jnp.pad(b, ((0, heads), (0, LANES))) + jnp.pad(c, ((0, heads), (LANES, 0)))
        + jnp.pad(codes.astype(F32), ((toks, 0), (0, 2 * LANES - toks)))
    )
    outs = pl.pallas_call(
        functools.partial(kernel, ctx, tp),
        out_shape=(
            shape(x.shape, F32), shape((toks // tp, LANES), F32),
            shape((toks // tp, LANES), F32), shape(codes.shape, F32),
        ),
        in_specs=[pl.BlockSpec(memory_space=pltpu.HBM)] * 2 + [vmem],
        out_specs=(vmem,) * 4,
        scratch_shapes=[
            pltpu.VMEM(x.shape, F32),
            pltpu.VMEM((2, pairs) + state, F32),
            pltpu.VMEM((pad, LANES), F32),
            pltpu.VMEM((pad, LANES), F32),
            pltpu.VMEM((pad, LANES), F32),
            pltpu.VMEM((pad, LANES), F32),
            pltpu.VMEM((2, hp) + state, F32),
            pltpu.VMEM((2, qp) + state, F32),
            pltpu.VMEM((2, qp) + state, F32),
            pltpu.VMEM((2, qp) + state, F32),
            pltpu.VMEM((2, qp) + state, F32),
            pltpu.VMEM((2, hp) + state, F32),
            pltpu.VMEM((2, qp) + state, F32),
            pltpu.VMEM((2, hp) + state, F32),
            pltpu.VMEM((2, pairs) + state, F32),
            pltpu.VMEM((toks, toks), F32),
            pltpu.VMEM((toks, toks), F32),
            pltpu.VMEM((-(-heads // 8) * 8, toks), F32),
            pltpu.VMEM((-(-heads // 8) * 8, toks), F32),
            pltpu.VMEM((-(-heads // 8) * 8, toks), F32),
            pltpu.VMEM((2, toks, LANES), F32),
            pltpu.VMEM((max(tp - 1, 1), 2, toks // tp, LANES), F32),
            pltpu.VMEM((toks, 2 * LANES), BF16),
            pltpu.VMEM((toks, 2 * LANES), BF16),
            pltpu.VMEM((2, pairs, toks, 2 * LANES), BF16),
            pltpu.VMEM(x.shape, F32),
            pltpu.VMEM(x.shape, F32),
            pltpu.SemaphoreType.DMA((copies,)),
            pltpu.SemaphoreType.DMA((copies,)),
            pltpu.SemaphoreType.DMA((8,)),
        ],
        compiler_params=pltpu.CompilerParams(
            collective_id=0, has_side_effects=True, vmem_limit_bytes=50 * 1024 * 1024
        ),
    )(x, g, small)
    return pl.pallas_call(
        store,
        out_shape=tuple(shape(one.shape, F32) for one in outs),
        in_specs=[vmem] * 4,
        out_specs=(pl.BlockSpec(memory_space=pltpu.HBM),) * 4,
        scratch_shapes=[pltpu.SemaphoreType.DMA((4,))],
        compiler_params=pltpu.CompilerParams(vmem_limit_bytes=8 * 1024 * 1024),
    )(*outs)


def solution(mesh):
    placed = (P("ctx", "tp"), P("ctx", None), P("ctx", None), P("tp", "ctx"), P("ctx", "tp"))
    return jax.shard_map(
        functools.partial(per_device, mesh.shape["ctx"], mesh.shape["tp"]),
        mesh=mesh,
        in_specs=placed,
        out_specs=(P("ctx", "tp"), P(("ctx", "tp"), None), P(("ctx", "tp"), None), P("tp", "ctx")),
        check_vma=False,
    )
```

```python
import functools

import jax
import jax.numpy as jnp
from jax import lax
from jax.experimental import pallas as pl
from jax.experimental.pallas import tpu as pltpu
from jax.sharding import PartitionSpec as P

MESH = pl.DeviceIdType.MESH
CODE_UNIT = 2.0 ** (-16)
LANES = 128
HALF = 64
F32 = jnp.float32
BF16 = jnp.bfloat16
NN = (((1,), (0,)), ((), ()))
NT = (((1,), (1,)), ((), ()))
TN = (((0,), (0,)), ((), ()))


def dot(a, b, dims=NN):
    return lax.dot_general(a, b, dims, preferred_element_type=F32)


def parts(a):
    high = a.astype(BF16)
    return high, (a - high.astype(F32)).astype(BF16)


def exact_dot(a, ones, dims):
    first = a.astype(BF16)
    rest = a - first.astype(F32)
    second = rest.astype(BF16)
    third = (rest - second.astype(F32)).astype(BF16)
    return dot(first, ones, dims) + dot(second, ones, dims) + dot(third, ones, dims)


def swap(a):
    return pltpu.roll(a, HALF, 1)


def kernel(
    ctx, tp, x_hbm, g_hbm, small_ref,
    dx_ref, db_ref, dc_ref, da_ref,
    wl, loc, dec, rdec0, dec1, rdec1, rbuf0, agg, rbuf1, zin, zout, zp, snd1, snd0, ent,
    score, dscore, w_rows, rows_acc, rowsq_acc, bc, rtp,
    cwide, bwide, wides, x_ref, g_ref, send, recv, fetched,
):
    heads, toks = da_ref.shape
    pairs = x_ref.shape[1] // LANES
    two = pairs % 2 == 0
    four = pairs % 4 == 0
    hp = pairs // 2 if two else pairs
    qp = pairs // 4 if four else hp
    group = 4 if four else 2 if two else 1
    groups = ctx // group
    mid = toks // 2

    me = lax.axis_index("ctx")
    my_tp = lax.axis_index("tp")
    place = me // group
    core = me % 2 if two else 0
    side = (me // 2) % 2 if four else 0
    core_mate = me + 1 - 2 * (me % 2)
    side_mate = me + 2 - 4 * ((me // 2) % 2)
    half0 = core * hp if two else 0
    mine0 = side * qp if four else 0

    if four:
        starts = [h * hp + s * qp for s in (1 - side, side) for h in (1 - core, core)]
    elif two:
        starts = [(1 - core) * hp, core * hp]
    else:
        starts = [0]

    def fetch(number):
        part, which = number // 2, number % 2
        src, dst = ((x_hbm, x_ref), (g_hbm, g_ref))[which]
        span = pl.ds(pl.multiple_of(starts[part] * LANES, LANES), qp * LANES)
        return pltpu.make_async_copy(src.at[:, span], dst.at[:, span], fetched.at[number])

    def arrived(*which):
        for part in which:
            fetch(2 * part).wait()
            fetch(2 * part + 1).wait()

    for number in range(2 * len(starts)):
        fetch(number).start()

    n_dec0 = 0
    n_dec1 = 1
    n_first = 2
    n_up = n_first + 2 * hp
    n_chain = n_up + 2 * qp
    n_down = n_chain + 2 * qp
    n_last = n_down + 2 * qp
    n_tp = n_last + 2 * hp

    def copy(src, dst, number, to):
        return pltpu.make_async_remote_copy(
            src_ref=src, dst_ref=dst, send_sem=send.at[number], recv_sem=recv.at[number],
            device_id=to, device_id_type=MESH,
        )

    def up0(d, k):
        return copy(
            loc.at[d, (1 - core) * hp + k], rbuf0.at[d, k], n_first + d * hp + k,
            {"ctx": core_mate},
        )

    def dec0_copy():
        return copy(dec, rdec0, n_dec0, {"ctx": core_mate})

    def dec1_copy():
        return copy(dec1, rdec1, n_dec1, {"ctx": side_mate})

    def up1(d, k):
        return copy(
            agg.at[d, k], rbuf1.at[d, k], n_up + d * qp + k, {"ctx": side_mate}
        )

    def chain(d, k):
        to = me + group if d == 0 else me - group
        return copy(zout.at[d, k], zin.at[d, k], n_chain + d * qp + k, {"ctx": to})

    def down1(d, k):
        return copy(
            snd1.at[d, k], zp.at[d, mine0 + k], n_down + d * qp + k, {"ctx": side_mate}
        )

    def down0(d, k):
        return copy(
            snd0.at[d, k], ent.at[d, half0 + k], n_last + d * hp + k, {"ctx": core_mate}
        )

    rt = toks // tp

    def tp_copy(step):
        to = lax.rem(my_tp + step, tp)
        return copy(
            bc.at[:, pl.ds(pl.multiple_of(to * rt, rt), rt)], rtp.at[step - 1],
            n_tp + step - 1, {"tp": to},
        )

    barrier = pltpu.get_barrier_semaphore()

    def greet(to):
        pl.semaphore_signal(barrier, inc=1, device_id=to, device_id_type=MESH)

    expected = tp - 1
    if two:
        greet({"ctx": core_mate})
        expected = expected + 1
    if four:
        greet({"ctx": side_mate})
        expected = expected + 1
    for step in range(1, tp):
        greet({"tp": lax.rem(my_tp + step, tp)})

    @pl.when(place > 0)
    def _():
        greet({"ctx": me - group})

    @pl.when(place < groups - 1)
    def _():
        greet({"ctx": me + group})

    inner = jnp.where(place > 0, 1, 0) + jnp.where(place < groups - 1, 1, 0)

    row_i = lax.broadcasted_iota(jnp.int32, (toks, toks), 0)
    col_i = lax.broadcasted_iota(jnp.int32, (toks, toks), 1)
    low_left = lax.broadcasted_iota(jnp.int32, (toks, LANES), 1) < HALF

    def cols(q):
        return pl.ds(pl.multiple_of(q * LANES, LANES), LANES)

    codes = small_ref[toks:toks + heads, 0:toks]
    code_high = jnp.floor(codes * (1.0 / 256.0))
    code_low = codes - code_high * 256.0
    upto = (col_i <= row_i).astype(BF16)
    run_high = dot(upto, code_high.astype(BF16), NT)
    run_low = dot(upto, code_low.astype(BF16), NT)
    total = run_high * 256.0 + run_low
    within_col = total * (-CODE_UNIT)

    w_rows[...] = jnp.zeros_like(w_rows)
    rows_acc[...] = jnp.zeros_like(rows_acc)
    rowsq_acc[...] = jnp.zeros_like(rowsq_acc)
    w_rows[0:heads, :] = (
        dot(code_high.astype(BF16), (row_i <= col_i).astype(BF16)) * 256.0
        + dot(code_low.astype(BF16), (row_i <= col_i).astype(BF16))
    ) * (-CODE_UNIT)
    for q in range(pairs):
        wl[:, q * LANES:(q + 1) * LANES] = jnp.where(
            low_left, within_col[:, 2 * q:2 * q + 1], within_col[:, 2 * q + 1:2 * q + 2]
        )
    dec[...] = jnp.zeros_like(dec)
    for q in range(pairs):
        dec[q:q + 1, :] = jnp.exp(wl[toks - 1:toks, q * LANES:(q + 1) * LANES])

    b_high, b_low = parts(small_ref[0:toks, :LANES])
    c_high, c_low = parts(small_ref[0:toks, LANES:])
    bwide[...] = jnp.concatenate([b_high, b_low], axis=1)
    cwide[...] = jnp.concatenate([c_high, c_low], axis=1)
    b_tall = jnp.transpose(jnp.concatenate([b_high.astype(F32), b_low.astype(F32)], axis=1)).astype(BF16)
    c_tall = jnp.transpose(jnp.concatenate([c_high.astype(F32), c_low.astype(F32)], axis=1)).astype(BF16)

    def weighted(q):
        w = wl[:, cols(q)]
        tail = jnp.exp(wl[pl.ds(toks - 1, 1), cols(q)] - w)
        return tail, jnp.exp(w)

    def local_state(q):
        tail, head = weighted(q)
        for d, (tall, value) in enumerate(
            ((b_tall, tail * x_ref[:, cols(q)]), (c_tall, head * g_ref[:, cols(q)]))
        ):
            high, low = parts(value)
            wide = jnp.concatenate([high, low], axis=1)
            wides[d, q] = wide
            out = dot(tall, wide)
            out = out[:LANES] + out[LANES:]
            loc[d, q] = out[:, :LANES] + out[:, LANES:]

    def loop(count, body):
        lax.fori_loop(0, count, lambda k, _: (body(k), 0)[1], 0)

    pl.semaphore_wait(barrier, expected + inner)

    def make(k):
        local_state((1 - core) * hp + k)
        local_state(half0 + k)
        for d in range(2):
            up0(d, k).start()

    def join(d, k):
        own_first = core == d
        q = half0 + k
        one = jnp.ones((1, LANES), F32)
        mine, other = dec[pl.ds(q, 1), :], rdec0[pl.ds(q, 1), :]
        up0(d, k).wait_recv()
        return (
            jnp.where(own_first, other, one) * loc[d, q]
            + jnp.where(own_first, one, mine) * rbuf0[d, k]
        )

    def pass_up(k):
        for d in range(2):
            agg[d, k] = join(d, (1 - side) * qp + k)
            up1(d, k).start()

    if two:
        dec0_copy().start()
        arrived(0, 1)
        other0 = (1 - side) * qp if four else 0
        make(other0)
        dec0_copy().wait()
        dec1[...] = dec[...] * rdec0[...]
        if four:
            dec1_copy().start()

            def step_up(k):
                make(other0 + k + 1)
                pass_up(k)

            loop(qp - 1, step_up)
            pass_up(qp - 1)
            arrived(2, 3)
            loop(qp, lambda k: make(mine0 + k))
        else:
            loop(qp - 1, lambda k: make(k + 1))
    else:
        arrived(0)
        loop(pairs, local_state)
        dec1[...] = dec[...]

    score[...] = (
        dot(b_high, c_high, NT) + dot(b_high, c_low, NT) + dot(b_low, c_high, NT)
    )
    dscore[...] = jnp.zeros_like(dscore)
    bc[...] = jnp.zeros_like(bc)
    dx_ref[...] = jnp.zeros_like(dx_ref)
    causal = row_i <= col_i

    def head_rows(a):
        turned = jnp.transpose(a)
        return [jnp.sum(turned[n * HALF:(n + 1) * HALF], axis=0, keepdims=True) for n in range(2)]

    def intra(*pair_list):
        pair_rows = [[w_rows[pl.ds(2 * q + n, 1), :] for n in range(2)] for q in pair_list]
        finished = []
        for q, w_row in zip(pair_list, pair_rows):
            x = x_ref[:, cols(q)]
            g = g_ref[:, cols(q)]
            w = wl[:, cols(q)]
            xh = x.astype(BF16).astype(F32)
            xl = x - xh
            gh = g.astype(BF16).astype(F32)
            gl = g - gh
            xl_s, gh_s, gl_s, w_s = swap(xl), swap(gh), swap(gl), swap(w)
            xh_b, gh_b = xh.astype(BF16), gh.astype(BF16)
            zero = jnp.zeros_like(g)
            results, folded, colsums = [], [], []
            for n in range(2):
                if n == 0:
                    pick = lambda a, b: jnp.where(low_left, a, b)
                else:
                    pick = lambda a, b: jnp.where(low_left, b, a)
                left = jnp.concatenate([pick(xh, xl_s).astype(BF16), xh_b], axis=1)
                right = jnp.concatenate(
                    [pick(gh, gh_s).astype(BF16), pick(gl, zero).astype(BF16)], axis=1
                )
                value = pick(gh, gl_s).astype(BF16)
                w_here = pick(w, w_s)
                dm = dot(left, right, NT)
                high, low, fold, colsum = [], [], [], []
                for r in range(2):
                    here = slice(r * mid, (r + 1) * mid)
                    after = slice(r * mid, toks)
                    width = toks - r * mid
                    wide = jnp.concatenate([w_here[here]] * (width // LANES), axis=1)
                    gap = jnp.where(causal[here, after], w_row[n][:, after] - wide, -1e30)
                    decay = jnp.exp(gap)
                    scaled = dm[here, after] * decay
                    sc = score[here, after]
                    dscore[here, after] += scaled
                    z = scaled * sc
                    colsum.append(jnp.sum(z, axis=0, keepdims=True))
                    fold.append(sum(z[:, i * LANES:(i + 1) * LANES] for i in range(width // LANES)))
                    mh, ml = parts(decay * sc)
                    if r:
                        nothing = jnp.zeros((mid, mid), BF16)
                        mh = jnp.concatenate([nothing, mh], axis=1)
                        ml = jnp.concatenate([nothing, ml], axis=1)
                    high.append(mh)
                    low.append(ml)
                main = dot(jnp.concatenate(high, axis=0), value)
                results.append(main + swap(main) + dot(jnp.concatenate(low, axis=0), gh_b))
                fold = jnp.concatenate(fold, axis=0)
                folded.append(fold + swap(fold))
                colsums.append(
                    jnp.concatenate([colsum[0][:, :mid], colsum[0][:, mid:] + colsum[1]], axis=1)
                )
            rowsums = head_rows(jnp.where(low_left, folded[0], folded[1]))
            finished.append((
                jnp.where(low_left, results[0], results[1]),
                [colsums[n] - rowsums[n] for n in range(2)],
            ))
        for q, (dx, rows) in zip(pair_list, finished):
            dx_ref[:, cols(q)] += dx
            for n in range(2):
                rows_acc[pl.ds(2 * q + n, 1), :] += rows[n]

    if four:
        dec1_copy().wait()

    def finish_core(d, k):
        q = half0 + k
        z = zp[d, k]
        if not two:
            ent[d, q] = z
            return
        own_first = core == d
        first_dec = jnp.where(own_first, dec[pl.ds(q, 1), :], rdec0[pl.ds(q, 1), :])
        first = jnp.where(own_first, loc[d, q], rbuf0[d, k])
        later = first_dec * z + first
        ent[d, q] = jnp.where(own_first, z, later)
        snd0[d, k] = jnp.where(own_first, later, z)
        down0(d, k).start()

    def carry(d, k):
        q = half0 + mine0 + k
        has_before = place > 0 if d == 0 else place < groups - 1
        has_after = place < groups - 1 if d == 0 else place > 0
        own = join(d, mine0 + k) if two else loc[d, k]
        mine = dec1[pl.ds(q, 1), :]
        if four:
            up1(d, k).wait_recv()
            other = rdec1[pl.ds(q, 1), :]
            got = rbuf1[d, k]
            own_first = side == d
            one = jnp.ones((1, LANES), F32)
            full = jnp.where(own_first, other, one) * own + jnp.where(own_first, one, mine) * got
            full_dec = mine * other
        else:
            full, full_dec = own, mine

        @pl.when(has_before)
        def _():
            chain(d, k).wait_recv()

        @pl.when(jnp.logical_not(has_before))
        def _():
            zin[d, k] = jnp.zeros((LANES, LANES), F32)

        z = zin[d, k]

        @pl.when(has_after)
        def _():
            zout[d, k] = full_dec * z + full
            chain(d, k).start()

        if four:
            first_dec = jnp.where(own_first, mine, other)
            later = first_dec * z + jnp.where(own_first, own, got)
            snd1[d, k] = jnp.where(own_first, later, z)
            down1(d, k).start()
            zp[d, mine0 + k] = jnp.where(own_first, z, later)
        else:
            zp[d, mine0 + k] = z
        finish_core(d, mine0 + k)

    ones_row = lax.broadcasted_iota(jnp.int32, (toks, LANES), 0) == toks - 1

    def inter_bc(*pair_list):
        db_sum, dc_sum = 0.0, 0.0
        for q in pair_list:
            s_tall = jnp.concatenate(parts(ent[0, q]), axis=0)
            g_tall = jnp.concatenate(parts(ent[1, q]), axis=0)
            dc_sum += dot(wides[1, q], jnp.concatenate([s_tall, s_tall], axis=1), NT)
            db_sum += dot(wides[0, q], jnp.concatenate([g_tall, g_tall], axis=1), NT)
        bc[0] += db_sum[:, :LANES] + db_sum[:, LANES:]
        bc[1] += dc_sum[:, :LANES] + dc_sum[:, LANES:]

    def inter_dx(*pair_list):
        finished = []
        for q in pair_list:
            tail = jnp.exp(wl[pl.ds(toks - 1, 1), cols(q)] - wl[:, cols(q)])
            tx, eg = wides[0, q], wides[1, q]
            s_wide = jnp.concatenate(parts(ent[0, q]), axis=1)
            g_wide = jnp.concatenate(parts(ent[1, q]), axis=1)
            y = dot(cwide[...], jnp.concatenate([s_wide, s_wide], axis=0))
            y = y[:, :LANES] + y[:, LANES:]
            dxi = dot(bwide[...], jnp.concatenate([g_wide, g_wide], axis=0))
            dxi = dxi[:, :LANES] + dxi[:, LANES:]
            across = jnp.sum(ent[0, q] * ent[1, q], axis=0, keepdims=True) * dec[pl.ds(q, 1), :]
            read = (eg[:, :LANES].astype(F32) + eg[:, LANES:].astype(F32)) * y
            read = read + jnp.where(ones_row, across, 0.0)
            wrote = (tx[:, :LANES].astype(F32) + tx[:, LANES:].astype(F32)) * dxi
            finished.append((tail * dxi, head_rows(read), head_rows(wrote)))
        for q, (dx, rows, rowsq) in zip(pair_list, finished):
            dx_ref[:, cols(q)] += dx
            for n in range(2):
                rows_acc[pl.ds(2 * q + n, 1), :] += rows[n]
                rowsq_acc[pl.ds(2 * q + n, 1), :] = rowsq[n]

    def inter(*pair_list):
        inter_bc(*pair_list)
        inter_dx(*pair_list)

    def within_block():
        dsh, dsl = parts(dscore[...])
        bc[0] += dot(dsh, c_high) + dot(dsh, c_low) + dot(dsl, c_high)
        bc[1] += dot(dsh, b_high, TN) + dot(dsh, b_low, TN) + dot(dsl, b_high, TN)

    both = jnp.maximum(place, groups - 1 - place)
    lag = 2 if four else 1 if two else 0
    intra_ticks = groups + 1
    per = -(-pairs // intra_ticks)
    ticks = groups - 1 + qp + lag

    def tick(t):
        def when_in(k, body):
            @pl.when(jnp.logical_and(k >= 0, k < qp))
            def _():
                body(k)

        for d in range(2):
            when_in(t - (place if d == 0 else groups - 1 - place), functools.partial(carry, d))
        now = t - both

        def side_in(k):
            for d in range(2):
                down1(d, k).wait_recv()
                finish_core(d, (1 - side) * qp + k)

        def core_wait(k):
            for d in range(2):
                down0(d, k).wait_recv()

        def first_three(k):
            core_wait(mine0 + k)
            inter(half0 + mine0 + k, half0 + (1 - side) * qp + k, (1 - core) * hp + mine0 + k)

        def last_one(k):
            core_wait((1 - side) * qp + k)
            inter_bc((1 - core) * hp + (1 - side) * qp + k)

        def first_two(k):
            core_wait(k)
            inter(half0 + k, (1 - core) * hp + k)

        if four:
            when_in(now - 1, side_in)
        q0 = t * per
        if pairs % per == 0:
            @pl.when(q0 < pairs)
            def _():
                for j in range(0, per, 2):
                    intra(*[q0 + i for i in range(j, min(j + 2, per))])
        else:
            for j in range(per):
                @pl.when(q0 + j < pairs)
                def _():
                    intra(q0 + j)

        if four:
            when_in(now - 1, first_three)
            when_in(now - 2, last_one)
        elif two:
            when_in(now - 1, first_two)
        else:
            when_in(now, inter)

        if ticks > intra_ticks:
            pl.when(t == intra_ticks)(within_block)

    loop(ticks, tick)
    if ticks <= intra_ticks:
        within_block()

    for step in range(1, tp):
        tp_copy(step).start()
    if four:
        inter_dx(*[(1 - core) * hp + (1 - side) * qp + k for k in range(qp)])

    later = (row_i >= col_i).astype(BF16)
    earlier = (row_i < col_i).astype(BF16)
    da_ref[...] = exact_dot(rows_acc[0:heads, :], later, NN) + exact_dot(
        rowsq_acc[0:heads, :], earlier, NN
    )

    own_rows = pl.ds(pl.multiple_of(my_tp * rt, rt), rt)
    db_sum = bc[0, own_rows]
    dc_sum = bc[1, own_rows]
    for step in range(1, tp):
        tp_copy(step).wait_recv()
        db_sum = db_sum + rtp[step - 1, 0]
        dc_sum = dc_sum + rtp[step - 1, 1]
    db_ref[...] = db_sum
    dc_ref[...] = dc_sum

    for step in range(1, tp):
        tp_copy(step).wait_send()

    def left(k):
        for d in range(2):
            has_after = place < groups - 1 if d == 0 else place > 0
            if four:
                up1(d, k).wait_send()
                down1(d, k).wait_send()

            @pl.when(has_after)
            def _():
                chain(d, k).wait_send()

    loop(qp, left)
    if two:
        def left_core(k):
            for d in range(2):
                up0(d, k).wait_send()
                down0(d, k).wait_send()

        loop(hp, left_core)


def store(*refs):
    done = refs[-1]
    half = (len(refs) - 1) // 2
    copies = [
        pltpu.make_async_copy(refs[n], refs[half + n], done.at[n]) for n in range(half)
    ]
    for one in copies:
        one.start()
    for one in copies:
        one.wait()


def per_device(ctx, tp, x, b, c, codes, g):
    heads, toks = codes.shape
    pairs = x.shape[1] // LANES
    hp = pairs // 2 if pairs % 2 == 0 else pairs
    qp = pairs // 4 if pairs % 4 == 0 else hp
    pad = -(-pairs // 8) * 8
    state = (LANES, LANES)
    copies = 2 + 6 * qp + 4 * hp + tp - 1
    vmem = pl.BlockSpec(memory_space=pltpu.VMEM)
    shape = jax.ShapeDtypeStruct
    small = (
        jnp.pad(b, ((0, heads), (0, LANES))) + jnp.pad(c, ((0, heads), (LANES, 0)))
        + jnp.pad(codes.astype(F32), ((toks, 0), (0, 2 * LANES - toks)))
    )
    outs = pl.pallas_call(
        functools.partial(kernel, ctx, tp),
        out_shape=(
            shape(x.shape, F32), shape((toks // tp, LANES), F32),
            shape((toks // tp, LANES), F32), shape(codes.shape, F32),
        ),
        in_specs=[pl.BlockSpec(memory_space=pltpu.HBM)] * 2 + [vmem],
        out_specs=(vmem,) * 4,
        scratch_shapes=[
            pltpu.VMEM(x.shape, F32),
            pltpu.VMEM((2, pairs) + state, F32),
            pltpu.VMEM((pad, LANES), F32),
            pltpu.VMEM((pad, LANES), F32),
            pltpu.VMEM((pad, LANES), F32),
            pltpu.VMEM((pad, LANES), F32),
            pltpu.VMEM((2, hp) + state, F32),
            pltpu.VMEM((2, qp) + state, F32),
            pltpu.VMEM((2, qp) + state, F32),
            pltpu.VMEM((2, qp) + state, F32),
            pltpu.VMEM((2, qp) + state, F32),
            pltpu.VMEM((2, hp) + state, F32),
            pltpu.VMEM((2, qp) + state, F32),
            pltpu.VMEM((2, hp) + state, F32),
            pltpu.VMEM((2, pairs) + state, F32),
            pltpu.VMEM((toks, toks), F32),
            pltpu.VMEM((toks, toks), F32),
            pltpu.VMEM((-(-heads // 8) * 8, toks), F32),
            pltpu.VMEM((-(-heads // 8) * 8, toks), F32),
            pltpu.VMEM((-(-heads // 8) * 8, toks), F32),
            pltpu.VMEM((2, toks, LANES), F32),
            pltpu.VMEM((max(tp - 1, 1), 2, toks // tp, LANES), F32),
            pltpu.VMEM((toks, 2 * LANES), BF16),
            pltpu.VMEM((toks, 2 * LANES), BF16),
            pltpu.VMEM((2, pairs, toks, 2 * LANES), BF16),
            pltpu.VMEM(x.shape, F32),
            pltpu.VMEM(x.shape, F32),
            pltpu.SemaphoreType.DMA((copies,)),
            pltpu.SemaphoreType.DMA((copies,)),
            pltpu.SemaphoreType.DMA((8,)),
        ],
        compiler_params=pltpu.CompilerParams(
            collective_id=0, has_side_effects=True, vmem_limit_bytes=50 * 1024 * 1024
        ),
    )(x, g, small)
    return pl.pallas_call(
        store,
        out_shape=tuple(shape(one.shape, F32) for one in outs),
        in_specs=[vmem] * 4,
        out_specs=(pl.BlockSpec(memory_space=pltpu.HBM),) * 4,
        scratch_shapes=[pltpu.SemaphoreType.DMA((4,))],
        compiler_params=pltpu.CompilerParams(vmem_limit_bytes=8 * 1024 * 1024),
    )(*outs)


def solution(mesh):
    placed = (P("ctx", "tp"), P("ctx", None), P("ctx", None), P("tp", "ctx"), P("ctx", "tp"))
    return jax.shard_map(
        functools.partial(per_device, mesh.shape["ctx"], mesh.shape["tp"]),
        mesh=mesh,
        in_specs=placed,
        out_specs=(P("ctx", "tp"), P(("ctx", "tp"), None), P(("ctx", "tp"), None), P("tp", "ctx")),
        check_vma=False,
    )
```

```python
import functools

import jax
import jax.numpy as jnp
from jax import lax
from jax.experimental import pallas as pl
from jax.experimental.pallas import tpu as pltpu
from jax.sharding import PartitionSpec as P

MESH = pl.DeviceIdType.MESH
CODE_UNIT = 2.0 ** (-16)
LANES = 128
HALF = 64
F32 = jnp.float32
BF16 = jnp.bfloat16
NN = (((1,), (0,)), ((), ()))
NT = (((1,), (1,)), ((), ()))
TN = (((0,), (0,)), ((), ()))


def dot(a, b, dims=NN):
    return lax.dot_general(a, b, dims, preferred_element_type=F32)


def parts(a):
    high = a.astype(BF16)
    return high, (a - high.astype(F32)).astype(BF16)


def exact_dot(a, ones, dims):
    first = a.astype(BF16)
    rest = a - first.astype(F32)
    second = rest.astype(BF16)
    third = (rest - second.astype(F32)).astype(BF16)
    return dot(first, ones, dims) + dot(second, ones, dims) + dot(third, ones, dims)


def swap(a):
    return pltpu.roll(a, HALF, 1)


def kernel(
    ctx, tp, x_hbm, g_hbm, small_ref, code_ref,
    dx_ref, db_ref, dc_ref, da_ref,
    wl, loc, dec, rdec0, dec1, rdec1, rbuf0, agg, rbuf1, zin, zout, zp, snd1, snd0, ent,
    score, dscore, w_rows, rows_acc, rowsq_acc, bc, rtp,
    cwide, bwide, wides, x_ref, g_ref, send, recv, fetched,
):
    heads, toks = da_ref.shape
    pairs = x_ref.shape[1] // LANES
    two = pairs % 2 == 0
    four = pairs % 4 == 0
    hp = pairs // 2 if two else pairs
    qp = pairs // 4 if four else hp
    group = 4 if four else 2 if two else 1
    groups = ctx // group
    mid = toks // 2

    me = lax.axis_index("ctx")
    my_tp = lax.axis_index("tp")
    place = me // group
    core = me % 2 if two else 0
    side = (me // 2) % 2 if four else 0
    core_mate = me + 1 - 2 * (me % 2)
    side_mate = me + 2 - 4 * ((me // 2) % 2)
    half0 = core * hp if two else 0
    mine0 = side * qp if four else 0

    if four:
        starts = [h * hp + s * qp for s in (1 - side, side) for h in (1 - core, core)]
    elif two:
        starts = [(1 - core) * hp, core * hp]
    else:
        starts = [0]

    def fetch(number):
        part, which = number // 2, number % 2
        src, dst = ((x_hbm, x_ref), (g_hbm, g_ref))[which]
        span = pl.ds(pl.multiple_of(starts[part] * LANES, LANES), qp * LANES)
        return pltpu.make_async_copy(src.at[:, span], dst.at[:, span], fetched.at[number])

    def arrived(*which):
        for part in which:
            fetch(2 * part).wait()
            fetch(2 * part + 1).wait()

    for number in range(2 * len(starts)):
        fetch(number).start()

    n_dec0 = 0
    n_dec1 = 1
    n_first = 2
    n_up = n_first + 2 * hp
    n_chain = n_up + 2 * qp
    n_down = n_chain + 2 * qp
    n_last = n_down + 2 * qp
    n_tp = n_last + 2 * hp

    def copy(src, dst, number, to):
        return pltpu.make_async_remote_copy(
            src_ref=src, dst_ref=dst, send_sem=send.at[number], recv_sem=recv.at[number],
            device_id=to, device_id_type=MESH,
        )

    def up0(d, k):
        return copy(
            loc.at[d, (1 - core) * hp + k], rbuf0.at[d, k], n_first + d * hp + k,
            {"ctx": core_mate},
        )

    def dec0_copy():
        return copy(dec, rdec0, n_dec0, {"ctx": core_mate})

    def dec1_copy():
        return copy(dec1, rdec1, n_dec1, {"ctx": side_mate})

    def up1(d, k):
        return copy(
            agg.at[d, k], rbuf1.at[d, k], n_up + d * qp + k, {"ctx": side_mate}
        )

    def chain(d, k):
        to = me + group if d == 0 else me - group
        return copy(zout.at[d, k], zin.at[d, k], n_chain + d * qp + k, {"ctx": to})

    def down1(d, k):
        return copy(
            snd1.at[d, k], zp.at[d, mine0 + k], n_down + d * qp + k, {"ctx": side_mate}
        )

    def down0(d, k):
        return copy(
            snd0.at[d, k], ent.at[d, half0 + k], n_last + d * hp + k, {"ctx": core_mate}
        )

    rt = toks // tp

    def tp_copy(step):
        to = lax.rem(my_tp + step, tp)
        return copy(
            bc.at[:, pl.ds(pl.multiple_of(to * rt, rt), rt)], rtp.at[step - 1],
            n_tp + step - 1, {"tp": to},
        )

    barrier = pltpu.get_barrier_semaphore()

    def greet(to):
        pl.semaphore_signal(barrier, inc=1, device_id=to, device_id_type=MESH)

    expected = tp - 1
    if two:
        greet({"ctx": core_mate})
        expected = expected + 1
    if four:
        greet({"ctx": side_mate})
        expected = expected + 1
    for step in range(1, tp):
        greet({"tp": lax.rem(my_tp + step, tp)})

    @pl.when(place > 0)
    def _():
        greet({"ctx": me - group})

    @pl.when(place < groups - 1)
    def _():
        greet({"ctx": me + group})

    inner = jnp.where(place > 0, 1, 0) + jnp.where(place < groups - 1, 1, 0)

    row_i = lax.broadcasted_iota(jnp.int32, (toks, toks), 0)
    col_i = lax.broadcasted_iota(jnp.int32, (toks, toks), 1)
    low_left = lax.broadcasted_iota(jnp.int32, (toks, LANES), 1) < HALF

    def cols(q):
        return pl.ds(pl.multiple_of(q * LANES, LANES), LANES)

    codes = code_ref[...]
    code_high = lax.shift_right_logical(codes, 8).astype(F32)
    code_low = (codes & 255).astype(F32)
    upto = (col_i <= row_i).astype(BF16)
    run_high = dot(upto, code_high.astype(BF16), NT)
    run_low = dot(upto, code_low.astype(BF16), NT)
    total = run_high * 256.0 + run_low
    within_col = total * (-CODE_UNIT)

    w_rows[...] = jnp.zeros_like(w_rows)
    rows_acc[...] = jnp.zeros_like(rows_acc)
    rowsq_acc[...] = jnp.zeros_like(rowsq_acc)
    w_rows[0:heads, :] = (
        dot(code_high.astype(BF16), (row_i <= col_i).astype(BF16)) * 256.0
        + dot(code_low.astype(BF16), (row_i <= col_i).astype(BF16))
    ) * (-CODE_UNIT)
    for q in range(pairs):
        wl[:, q * LANES:(q + 1) * LANES] = jnp.where(
            low_left, within_col[:, 2 * q:2 * q + 1], within_col[:, 2 * q + 1:2 * q + 2]
        )
    dec[...] = jnp.zeros_like(dec)
    for q in range(pairs):
        dec[q:q + 1, :] = jnp.exp(wl[toks - 1:toks, q * LANES:(q + 1) * LANES])

    b_high, b_low = parts(small_ref[0:toks, :LANES])
    c_high, c_low = parts(small_ref[0:toks, LANES:])
    bwide[...] = jnp.concatenate([b_high, b_low], axis=1)
    cwide[...] = jnp.concatenate([c_high, c_low], axis=1)
    b_tall = jnp.transpose(jnp.concatenate([b_high.astype(F32), b_low.astype(F32)], axis=1)).astype(BF16)
    c_tall = jnp.transpose(jnp.concatenate([c_high.astype(F32), c_low.astype(F32)], axis=1)).astype(BF16)

    def weighted(q):
        w = wl[:, cols(q)]
        tail = jnp.exp(wl[pl.ds(toks - 1, 1), cols(q)] - w)
        return tail, jnp.exp(w)

    def local_state(q):
        tail, head = weighted(q)
        for d, (tall, value) in enumerate(
            ((b_tall, tail * x_ref[:, cols(q)]), (c_tall, head * g_ref[:, cols(q)]))
        ):
            high, low = parts(value)
            wide = jnp.concatenate([high, low], axis=1)
            wides[d, q] = wide
            out = dot(tall, wide)
            out = out[:LANES] + out[LANES:]
            loc[d, q] = out[:, :LANES] + out[:, LANES:]

    def loop(count, body):
        lax.fori_loop(0, count, lambda k, _: (body(k), 0)[1], 0)

    pl.semaphore_wait(barrier, expected + inner)

    def make(k):
        local_state((1 - core) * hp + k)
        local_state(half0 + k)
        for d in range(2):
            up0(d, k).start()

    def join(d, k):
        own_first = core == d
        q = half0 + k
        one = jnp.ones((1, LANES), F32)
        mine, other = dec[pl.ds(q, 1), :], rdec0[pl.ds(q, 1), :]
        up0(d, k).wait_recv()
        return (
            jnp.where(own_first, other, one) * loc[d, q]
            + jnp.where(own_first, one, mine) * rbuf0[d, k]
        )

    def pass_up(k):
        for d in range(2):
            agg[d, k] = join(d, (1 - side) * qp + k)
            up1(d, k).start()

    if two:
        dec0_copy().start()
        arrived(0, 1)
        other0 = (1 - side) * qp if four else 0
        make(other0)
        dec0_copy().wait()
        dec1[...] = dec[...] * rdec0[...]
        if four:
            dec1_copy().start()

            def step_up(k):
                make(other0 + k + 1)
                pass_up(k)

            loop(qp - 1, step_up)
            pass_up(qp - 1)
            arrived(2, 3)
            loop(qp, lambda k: make(mine0 + k))
        else:
            loop(qp - 1, lambda k: make(k + 1))
    else:
        arrived(0)
        loop(pairs, local_state)
        dec1[...] = dec[...]

    score[...] = (
        dot(b_high, c_high, NT) + dot(b_high, c_low, NT) + dot(b_low, c_high, NT)
    )
    dscore[...] = jnp.zeros_like(dscore)
    bc[...] = jnp.zeros_like(bc)
    dx_ref[...] = jnp.zeros_like(dx_ref)
    causal = row_i <= col_i

    def head_rows(a):
        turned = jnp.transpose(a)
        return [jnp.sum(turned[n * HALF:(n + 1) * HALF], axis=0, keepdims=True) for n in range(2)]

    def intra(*pair_list):
        pair_rows = [[w_rows[pl.ds(2 * q + n, 1), :] for n in range(2)] for q in pair_list]
        finished = []
        for q, w_row in zip(pair_list, pair_rows):
            x = x_ref[:, cols(q)]
            g = g_ref[:, cols(q)]
            w = wl[:, cols(q)]
            xh = x.astype(BF16).astype(F32)
            xl = x - xh
            gh = g.astype(BF16).astype(F32)
            gl = g - gh
            xl_s, gl_s, w_s = swap(xl), swap(gl), swap(w)
            gh_t = jnp.transpose(gh).astype(BF16)
            gl_t = jnp.transpose(gl).astype(BF16)
            xh_b, gh_b = xh.astype(BF16), gh.astype(BF16)
            zero = jnp.zeros((HALF, toks), BF16)
            results, folded, colsums = [], [], []
            for n in range(2):
                if n == 0:
                    pick = lambda a, b: jnp.where(low_left, a, b)
                else:
                    pick = lambda a, b: jnp.where(low_left, b, a)
                left = jnp.concatenate([pick(xh, xl_s).astype(BF16), xh_b], axis=1)
                own = slice(n * HALF, (n + 1) * HALF)
                ends = [gl_t[own], zero] if n == 0 else [zero, gl_t[own]]
                right = jnp.concatenate([gh_t[own], gh_t[own]] + ends, axis=0)
                value = pick(gh, gl_s).astype(BF16)
                w_here = pick(w, w_s)
                dm = dot(left, right)
                high, low, fold, colsum = [], [], [], []
                for r in range(2):
                    here = slice(r * mid, (r + 1) * mid)
                    after = slice(r * mid, toks)
                    width = toks - r * mid
                    wide = jnp.concatenate([w_here[here]] * (width // LANES), axis=1)
                    gap = jnp.where(causal[here, after], w_row[n][:, after] - wide, -1e30)
                    decay = jnp.exp(gap)
                    scaled = dm[here, after] * decay
                    sc = score[here, after]
                    dscore[here, after] += scaled
                    z = scaled * sc
                    colsum.append(jnp.sum(z, axis=0, keepdims=True))
                    fold.append(sum(z[:, i * LANES:(i + 1) * LANES] for i in range(width // LANES)))
                    mh, ml = parts(decay * sc)
                    if r:
                        nothing = jnp.zeros((mid, mid), BF16)
                        mh = jnp.concatenate([nothing, mh], axis=1)
                        ml = jnp.concatenate([nothing, ml], axis=1)
                    high.append(mh)
                    low.append(ml)
                main = dot(jnp.concatenate(high, axis=0), value)
                results.append(main + swap(main) + dot(jnp.concatenate(low, axis=0), gh_b))
                fold = jnp.concatenate(fold, axis=0)
                folded.append(fold + swap(fold))
                colsums.append(
                    jnp.concatenate([colsum[0][:, :mid], colsum[0][:, mid:] + colsum[1]], axis=1)
                )
            rowsums = head_rows(jnp.where(low_left, folded[0], folded[1]))
            finished.append((
                jnp.where(low_left, results[0], results[1]),
                [colsums[n] - rowsums[n] for n in range(2)],
            ))
        for q, (dx, rows) in zip(pair_list, finished):
            dx_ref[:, cols(q)] += dx
            for n in range(2):
                rows_acc[pl.ds(2 * q + n, 1), :] += rows[n]

    if four:
        dec1_copy().wait()

    def finish_core(d, k):
        q = half0 + k
        z = zp[d, k]
        if not two:
            ent[d, q] = z
            return
        own_first = core == d
        first_dec = jnp.where(own_first, dec[pl.ds(q, 1), :], rdec0[pl.ds(q, 1), :])
        first = jnp.where(own_first, loc[d, q], rbuf0[d, k])
        later = first_dec * z + first
        ent[d, q] = jnp.where(own_first, z, later)
        snd0[d, k] = jnp.where(own_first, later, z)
        down0(d, k).start()

    def carry(d, k):
        q = half0 + mine0 + k
        has_before = place > 0 if d == 0 else place < groups - 1
        has_after = place < groups - 1 if d == 0 else place > 0
        own = join(d, mine0 + k) if two else loc[d, k]
        mine = dec1[pl.ds(q, 1), :]
        if four:
            up1(d, k).wait_recv()
            other = rdec1[pl.ds(q, 1), :]
            got = rbuf1[d, k]
            own_first = side == d
            one = jnp.ones((1, LANES), F32)
            full = jnp.where(own_first, other, one) * own + jnp.where(own_first, one, mine) * got
            full_dec = mine * other
        else:
            full, full_dec = own, mine

        @pl.when(has_before)
        def _():
            chain(d, k).wait_recv()

        @pl.when(jnp.logical_not(has_before))
        def _():
            zin[d, k] = jnp.zeros((LANES, LANES), F32)

        z = zin[d, k]

        @pl.when(has_after)
        def _():
            zout[d, k] = full_dec * z + full
            chain(d, k).start()

        if four:
            first_dec = jnp.where(own_first, mine, other)
            later = first_dec * z + jnp.where(own_first, own, got)
            snd1[d, k] = jnp.where(own_first, later, z)
            down1(d, k).start()
            zp[d, mine0 + k] = jnp.where(own_first, z, later)
        else:
            zp[d, mine0 + k] = z
        finish_core(d, mine0 + k)

    ones_row = lax.broadcasted_iota(jnp.int32, (toks, LANES), 0) == toks - 1

    def inter_bc(*pair_list):
        db_sum, dc_sum = 0.0, 0.0
        for q in pair_list:
            s_tall = jnp.concatenate(parts(ent[0, q]), axis=0)
            g_tall = jnp.concatenate(parts(ent[1, q]), axis=0)
            dc_sum += dot(wides[1, q], jnp.concatenate([s_tall, s_tall], axis=1), NT)
            db_sum += dot(wides[0, q], jnp.concatenate([g_tall, g_tall], axis=1), NT)
        bc[0] += db_sum[:, :LANES] + db_sum[:, LANES:]
        bc[1] += dc_sum[:, :LANES] + dc_sum[:, LANES:]

    def inter_dx(*pair_list):
        finished = []
        for q in pair_list:
            tail = jnp.exp(wl[pl.ds(toks - 1, 1), cols(q)] - wl[:, cols(q)])
            tx, eg = wides[0, q], wides[1, q]
            s_wide = jnp.concatenate(parts(ent[0, q]), axis=1)
            g_wide = jnp.concatenate(parts(ent[1, q]), axis=1)
            y = dot(cwide[...], jnp.concatenate([s_wide, s_wide], axis=0))
            y = y[:, :LANES] + y[:, LANES:]
            dxi = dot(bwide[...], jnp.concatenate([g_wide, g_wide], axis=0))
            dxi = dxi[:, :LANES] + dxi[:, LANES:]
            across = jnp.sum(ent[0, q] * ent[1, q], axis=0, keepdims=True) * dec[pl.ds(q, 1), :]
            read = (eg[:, :LANES].astype(F32) + eg[:, LANES:].astype(F32)) * y
            read = read + jnp.where(ones_row, across, 0.0)
            wrote = (tx[:, :LANES].astype(F32) + tx[:, LANES:].astype(F32)) * dxi
            finished.append((tail * dxi, head_rows(read), head_rows(wrote)))
        for q, (dx, rows, rowsq) in zip(pair_list, finished):
            dx_ref[:, cols(q)] += dx
            for n in range(2):
                rows_acc[pl.ds(2 * q + n, 1), :] += rows[n]
                rowsq_acc[pl.ds(2 * q + n, 1), :] = rowsq[n]

    def inter(*pair_list):
        inter_bc(*pair_list)
        inter_dx(*pair_list)

    def within_block():
        dsh, dsl = parts(dscore[...])
        bc[0] += dot(dsh, c_high) + dot(dsh, c_low) + dot(dsl, c_high)
        bc[1] += dot(dsh, b_high, TN) + dot(dsh, b_low, TN) + dot(dsl, b_high, TN)

    both = jnp.maximum(place, groups - 1 - place)
    lag = 2 if four else 1 if two else 0
    intra_ticks = groups + 1
    per = -(-pairs // intra_ticks)
    ticks = groups - 1 + qp + lag

    def tick(t):
        def when_in(k, body):
            @pl.when(jnp.logical_and(k >= 0, k < qp))
            def _():
                body(k)

        for d in range(2):
            when_in(t - (place if d == 0 else groups - 1 - place), functools.partial(carry, d))
        now = t - both

        def side_in(k):
            for d in range(2):
                down1(d, k).wait_recv()
                finish_core(d, (1 - side) * qp + k)

        def core_wait(k):
            for d in range(2):
                down0(d, k).wait_recv()

        def first_three(k):
            core_wait(mine0 + k)
            inter(half0 + mine0 + k, half0 + (1 - side) * qp + k, (1 - core) * hp + mine0 + k)

        def last_one(k):
            core_wait((1 - side) * qp + k)
            inter_bc((1 - core) * hp + (1 - side) * qp + k)

        def first_two(k):
            core_wait(k)
            inter(half0 + k, (1 - core) * hp + k)

        if four:
            when_in(now - 1, side_in)
        q0 = t * per
        if pairs % per == 0:
            @pl.when(q0 < pairs)
            def _():
                for j in range(0, per, 2):
                    intra(*[q0 + i for i in range(j, min(j + 2, per))])
        else:
            for j in range(per):
                @pl.when(q0 + j < pairs)
                def _():
                    intra(q0 + j)

        if four:
            when_in(now - 1, first_three)
            when_in(now - 2, last_one)
        elif two:
            when_in(now - 1, first_two)
        else:
            when_in(now, inter)

        if ticks > intra_ticks:
            pl.when(t == intra_ticks)(within_block)

    loop(ticks, tick)
    if ticks <= intra_ticks:
        within_block()

    for step in range(1, tp):
        tp_copy(step).start()
    if four:
        inter_dx(*[(1 - core) * hp + (1 - side) * qp + k for k in range(qp)])

    later = (row_i >= col_i).astype(BF16)
    earlier = (row_i < col_i).astype(BF16)
    da_ref[...] = exact_dot(rows_acc[0:heads, :], later, NN) + exact_dot(
        rowsq_acc[0:heads, :], earlier, NN
    )

    own_rows = pl.ds(pl.multiple_of(my_tp * rt, rt), rt)
    db_sum = bc[0, own_rows]
    dc_sum = bc[1, own_rows]
    for step in range(1, tp):
        tp_copy(step).wait_recv()
        db_sum = db_sum + rtp[step - 1, 0]
        dc_sum = dc_sum + rtp[step - 1, 1]
    db_ref[...] = db_sum
    dc_ref[...] = dc_sum

    for step in range(1, tp):
        tp_copy(step).wait_send()

    def left(k):
        for d in range(2):
            has_after = place < groups - 1 if d == 0 else place > 0
            if four:
                up1(d, k).wait_send()
                down1(d, k).wait_send()

            @pl.when(has_after)
            def _():
                chain(d, k).wait_send()

    loop(qp, left)
    if two:
        def left_core(k):
            for d in range(2):
                up0(d, k).wait_send()
                down0(d, k).wait_send()

        loop(hp, left_core)


def store(*refs):
    done = refs[-1]
    half = (len(refs) - 1) // 2
    copies = [
        pltpu.make_async_copy(refs[n], refs[half + n], done.at[n]) for n in range(half)
    ]
    for one in copies:
        one.start()
    for one in copies:
        one.wait()


def per_device(ctx, tp, x, b, c, codes, g):
    heads, toks = codes.shape
    pairs = x.shape[1] // LANES
    hp = pairs // 2 if pairs % 2 == 0 else pairs
    qp = pairs // 4 if pairs % 4 == 0 else hp
    pad = -(-pairs // 8) * 8
    state = (LANES, LANES)
    copies = 2 + 6 * qp + 4 * hp + tp - 1
    vmem = pl.BlockSpec(memory_space=pltpu.VMEM)
    shape = jax.ShapeDtypeStruct
    small = jnp.concatenate([b, c], axis=1)
    outs = pl.pallas_call(
        functools.partial(kernel, ctx, tp),
        out_shape=(
            shape(x.shape, F32), shape((toks // tp, LANES), F32),
            shape((toks // tp, LANES), F32), shape(codes.shape, F32),
        ),
        in_specs=[pl.BlockSpec(memory_space=pltpu.HBM)] * 2 + [vmem] * 2,
        out_specs=(vmem,) * 4,
        scratch_shapes=[
            pltpu.VMEM(x.shape, F32),
            pltpu.VMEM((2, pairs) + state, F32),
            pltpu.VMEM((pad, LANES), F32),
            pltpu.VMEM((pad, LANES), F32),
            pltpu.VMEM((pad, LANES), F32),
            pltpu.VMEM((pad, LANES), F32),
            pltpu.VMEM((2, hp) + state, F32),
            pltpu.VMEM((2, qp) + state, F32),
            pltpu.VMEM((2, qp) + state, F32),
            pltpu.VMEM((2, qp) + state, F32),
            pltpu.VMEM((2, qp) + state, F32),
            pltpu.VMEM((2, hp) + state, F32),
            pltpu.VMEM((2, qp) + state, F32),
            pltpu.VMEM((2, hp) + state, F32),
            pltpu.VMEM((2, pairs) + state, F32),
            pltpu.VMEM((toks, toks), F32),
            pltpu.VMEM((toks, toks), F32),
            pltpu.VMEM((-(-heads // 8) * 8, toks), F32),
            pltpu.VMEM((-(-heads // 8) * 8, toks), F32),
            pltpu.VMEM((-(-heads // 8) * 8, toks), F32),
            pltpu.VMEM((2, toks, LANES), F32),
            pltpu.VMEM((max(tp - 1, 1), 2, toks // tp, LANES), F32),
            pltpu.VMEM((toks, 2 * LANES), BF16),
            pltpu.VMEM((toks, 2 * LANES), BF16),
            pltpu.VMEM((2, pairs, toks, 2 * LANES), BF16),
            pltpu.VMEM(x.shape, F32),
            pltpu.VMEM(x.shape, F32),
            pltpu.SemaphoreType.DMA((copies,)),
            pltpu.SemaphoreType.DMA((copies,)),
            pltpu.SemaphoreType.DMA((8,)),
        ],
        compiler_params=pltpu.CompilerParams(
            collective_id=0, has_side_effects=True, vmem_limit_bytes=50 * 1024 * 1024
        ),
    )(x, g, small, codes)
    return pl.pallas_call(
        store,
        out_shape=tuple(shape(one.shape, F32) for one in outs),
        in_specs=[vmem] * 4,
        out_specs=(pl.BlockSpec(memory_space=pltpu.HBM),) * 4,
        scratch_shapes=[pltpu.SemaphoreType.DMA((4,))],
        compiler_params=pltpu.CompilerParams(vmem_limit_bytes=8 * 1024 * 1024),
    )(*outs)


def solution(mesh):
    placed = (P("ctx", "tp"), P("ctx", None), P("ctx", None), P("tp", "ctx"), P("ctx", "tp"))
    return jax.shard_map(
        functools.partial(per_device, mesh.shape["ctx"], mesh.shape["tp"]),
        mesh=mesh,
        in_specs=placed,
        out_specs=(P("ctx", "tp"), P(("ctx", "tp"), None), P(("ctx", "tp"), None), P("tp", "ctx")),
        check_vma=False,
    )
```
